32 devices in a mesh: mesh: 8 (over z, x), lev: 4 (over y, core).
Axes of the slice: x: 2, y: 2, z: 4, core: 2. Of those that a mesh axis runs over, the one named last changes fastest.
Arguments:
- velocity: float32 [8, 24576], P('lev', 'mesh'), may hold values from -6 to 6
- thickness: float32 [8, 24576], P('lev', 'mesh'), may hold values from 0.5 to 2
- vorticity: float32 [8, 24576], P('lev', 'mesh'), may hold values from -6 to 6
- vertical_wind: float32 [8, 24576], P('lev', 'mesh'), may hold values from -6 to 6
- weights_on_edge: float32 [10, 24576], P(None, 'mesh'), may hold values from -2 to 2
- edges_on_edge: int32 [10, 24576], P(None, 'mesh'), may hold values from 0 to 3839, as said below
- edges_on_cell: int32 [6, 8192], P(None, 'mesh'), may hold values from 0 to 3839, as said below
- cells_on_edge: int32 [2, 24576], P(None, 'mesh'), may hold values from 0 to 1407, as said below
- energy_weight: float32 [6, 8192], P(None, 'mesh'), may hold values from 0.05 to 0.5
- inverse_distance: float32 [24576], P('mesh'), may hold values from 0.5 to 2
- edge_halo_list: int32 [48, 128], P('mesh'), may hold values from 0 to 3071
- edge_halo_count: int32 [48], P('mesh'), may hold values from 1 to 128, as said below
- cell_halo_list: int32 [48, 64], P('mesh'), may hold values from 0 to 1023
- cell_halo_count: int32 [48], P('mesh'), may hold values from 1 to 64, as said below
Outputs:
- tendency: float32 [8, 24576], P('lev', 'mesh')
- tangent: float32 [8, 24576], P('lev', 'mesh')
- energy: float32 [8, 8192], P('lev', 'mesh')
The draws below stay inside these ranges and needn't reach their ends.
Inputs may be any that keep to these rules, and one draw needn't show every extreme that they name: `edge_halo_count`: row r names how many leading slots of the halo block r are live. `cell_halo_count`: row r names how many leading slots of the halo block r are live. `edges_on_edge`: entries name local edges or live slots of edge halo blocks. `edges_on_cell`: entries name local edges or live slots of edge halo blocks. `cells_on_edge`: entries name local cells or live slots of cell halo blocks.
All inputs are finite; a program needn't handle non-finite values.
Results may differ from the reference program's by a relative error of at most 0.0003.
Values sent between devices are 32-bit elements; how exact they have to be, the bound alone decides.
A program may use at most 128 MiB of HBM per device.

```python
import math
import jax
import jax.numpy as jnp
from jax import lax

C_DEV = 1024
E_DEV = 3072
NEOE = 10
NEOC = 6
REACH = 3
HALO_E = 128
HALO_C = 64
NBLOCK = 6
NLEV = 8
EDGES = 24576
CELLS = 8192
N_MESH = 8


def offsets_table_drawn():
    order = jnp.arange(NBLOCK, dtype=jnp.int32)
    return jnp.where(order < REACH, order + 1, REACH - 1 - order).astype(jnp.int32)


def halo_counts(key, salt, most):
    inner = jax.random.fold_in(key, salt)
    first, second = jax.random.split(inner)
    counts = jax.random.randint(first, (N_MESH * NBLOCK,), 1, most + 1)
    sender = jax.random.randint(second, (), 0, N_MESH)
    full_row = sender * NBLOCK + NBLOCK - 1
    counts = jnp.where(jnp.arange(N_MESH * NBLOCK) == full_row, most, counts)
    return (counts.astype(jnp.int32), sender)


def halo_refs(key, total, local_size, column_size, counts, sender, most, leading):
    keys = jax.random.split(key, 4)
    owner = (jnp.arange(total, dtype=jnp.int32) // column_size)[None, :]
    local_pick = jax.random.randint(keys[0], (leading, total), 0, local_size)
    block = jax.random.randint(keys[1], (leading, total), 0, NBLOCK)
    raw_slot = jax.random.randint(keys[2], (leading, total), 0, 1 << 20)
    remote = jax.random.randint(keys[3], (leading, total), 0, 4) == 0
    source = (owner - offsets_table_drawn()[block]) % N_MESH
    live = counts[source * NBLOCK + block]
    slot = raw_slot % live
    table = jnp.where(remote, local_size + block * most + slot, local_pick)
    receiver = (sender - REACH) % N_MESH
    spot = (jnp.arange(leading)[:, None] == 0) & (jnp.arange(total)[None, :] == receiver * column_size)
    table = jnp.where(spot, local_size + NBLOCK * most - 1, table)
    return table.astype(jnp.int32)


def bounded_list(key, rows, breadth, top):
    keys = jax.random.split(key, 3)
    values = jax.random.randint(keys[0], (rows * breadth,), 0, top)
    high_spot = jax.random.randint(keys[1], (), 0, rows * breadth)
    low_spot = (high_spot + 1 + jax.random.randint(keys[2], (), 0, rows * breadth - 1)) % (rows * breadth)
    places = jnp.arange(rows * breadth)
    values = jnp.where(places == high_spot, top - 1, values)
    values = jnp.where(places == low_spot, 0, values)
    return values.reshape(rows, breadth).astype(jnp.int32)


def draw_edge_halo_count(key, part):
    counts, sender = halo_counts(key, 11, HALO_E)
    return counts


def draw_cell_halo_count(key, part):
    counts, sender = halo_counts(key, 12, HALO_C)
    return counts


def draw_edge_halo_list(key, part):
    key = jax.random.fold_in(key, 21)
    return bounded_list(key, N_MESH * NBLOCK, HALO_E, E_DEV)


def draw_cell_halo_list(key, part):
    key = jax.random.fold_in(key, 22)
    return bounded_list(key, N_MESH * NBLOCK, HALO_C, C_DEV)


def draw_edges_on_edge(key, part):
    counts, sender = halo_counts(key, 11, HALO_E)
    key = jax.random.fold_in(key, 31)
    return halo_refs(key, EDGES, E_DEV, E_DEV, counts, sender, HALO_E, NEOE)


def draw_edges_on_cell(key, part):
    counts, sender = halo_counts(key, 11, HALO_E)
    key = jax.random.fold_in(key, 32)
    return halo_refs(key, CELLS, E_DEV, C_DEV, counts, sender, HALO_E, NEOC)


def draw_cells_on_edge(key, part):
    counts, sender = halo_counts(key, 12, HALO_C)
    key = jax.random.fold_in(key, 33)
    return halo_refs(key, EDGES, C_DEV, E_DEV, counts, sender, HALO_C, 2)


def block_levels(key, shape, pieces, smallest, top_value):
    loudness = 1.0
    for position, shards_of in pieces:
        draws = jax.random.uniform(jax.random.fold_in(jax.random.fold_in(key, 6), position), (shards_of,), jnp.float32, smallest / len(pieces), top_value / len(pieces))
        loudness = loudness * jnp.repeat(jnp.exp(draws), shape[position] // shards_of).reshape((-1,) + (1,) * (len(shape) - 1 - position))
    return loudness


def normal_values(stream_key, dims, width, most, cuts=(), kind=jnp.bfloat16):
    array = jax.random.normal(stream_key, dims, jnp.float32) * width
    if len(cuts) > 0:
        array = block_levels(stream_key, dims, cuts, -0.22, 0.18) * array
    return jnp.clip(array, min=-most, max=most).astype(kind)


def setup_inputs(seed: int = 0) -> dict:
    key_of = jax.random.split(jax.random.key(seed), 15)
    return {
        "velocity": normal_values(key_of[0], (NLEV, EDGES), 1.0, 6.0, ((0, 4), (1, 8)), jnp.float32),
        "thickness": jnp.clip(jnp.exp(math.log(2.0) - 1.3862944 * jax.random.uniform(key_of[1], (NLEV, EDGES), jnp.float32) ** block_levels(key_of[1], (NLEV, EDGES), ((0, 4), (1, 8)), -0.2, 0.2)), 0.5, 2.0),
        "vorticity": normal_values(key_of[2], (NLEV, EDGES), 1.0, 6.0, ((0, 4), (1, 8)), jnp.float32),
        "vertical_wind": normal_values(key_of[3], (NLEV, EDGES), 1.0, 6.0, ((0, 4), (1, 8)), jnp.float32),
        "weights_on_edge": normal_values(key_of[4], (NEOE, EDGES), NEOE ** -0.5, 2.0, ((1, 8),), jnp.float32),
        "edges_on_edge": draw_edges_on_edge(jax.random.fold_in(key_of[14], 71), 0),
        "edges_on_cell": draw_edges_on_cell(jax.random.fold_in(key_of[14], 71), 0),
        "cells_on_edge": draw_cells_on_edge(jax.random.fold_in(key_of[14], 71), 0),
        "energy_weight": jnp.clip(jnp.exp(math.log(0.5) - 2.3025851 * jax.random.uniform(key_of[8], (NEOC, CELLS), jnp.float32) ** block_levels(key_of[8], (NEOC, CELLS), ((1, 8),), -0.2, 0.2)), 0.05, 0.5),
        "inverse_distance": jnp.clip(jnp.exp(math.log(2.0) - 1.3862944 * jax.random.uniform(key_of[9], (EDGES,), jnp.float32) ** block_levels(key_of[9], (EDGES,), ((0, 8),), -0.2, 0.2)), 0.5, 2.0),
        "edge_halo_list": draw_edge_halo_list(jax.random.fold_in(key_of[14], 71), 0),
        "edge_halo_count": draw_edge_halo_count(jax.random.fold_in(key_of[14], 71), 0),
        "cell_halo_list": draw_cell_halo_list(jax.random.fold_in(key_of[14], 71), 0),
        "cell_halo_count": draw_cell_halo_count(jax.random.fold_in(key_of[14], 71), 0),
    }


def offsets_table():
    order = jnp.arange(NBLOCK, dtype=jnp.int32)
    return jnp.where(order < REACH, order + 1, REACH - 1 - order).astype(jnp.int32)


def resolve(table, local_size, column_size, halo_list, halo_count, breadth):
    total = table.shape[-1]
    owner = (jnp.arange(total, dtype=jnp.int32) // column_size)[None, :]
    slot = jnp.maximum(table - local_size, 0)
    block = slot // breadth
    place = slot % breadth
    sender = (owner - offsets_table()[block]) % N_MESH
    row = (sender * NBLOCK + block).astype(jnp.int32)
    remote_item = sender * local_size + halo_list[row, place]
    remote = table >= local_size
    index = jnp.where(remote, remote_item, owner * local_size + table).astype(jnp.int32)
    keep = jnp.where(remote, place < halo_count[row], True)
    return index, keep


def reference(velocity, thickness, vorticity, vertical_wind, weights_on_edge, edges_on_edge, edges_on_cell, cells_on_edge, energy_weight, inverse_distance, edge_halo_list, edge_halo_count, cell_halo_list, cell_halo_count):
    near_edges, near_keep = resolve(edges_on_edge, E_DEV, E_DEV, edge_halo_list, edge_halo_count, HALO_E)
    cell_edges, cell_keep = resolve(edges_on_cell, E_DEV, C_DEV, edge_halo_list, edge_halo_count, HALO_E)
    end_cells, end_keep = resolve(cells_on_edge, C_DEV, E_DEV, cell_halo_list, cell_halo_count, HALO_C)

    def level_terms(row):
        speed, height, potential = row
        speed_near = jnp.where(near_keep, speed[near_edges], 0.0)
        height_near = jnp.where(near_keep, height[near_edges], 0.0)
        potential_near = jnp.where(near_keep, potential[near_edges], 0.0)
        tangent_row = jnp.sum(weights_on_edge * speed_near, axis=0)
        flux_row = jnp.sum(weights_on_edge * speed_near * height_near * 0.5 * (potential[None, :] + potential_near), axis=0)
        cell_speed = jnp.where(cell_keep, speed[cell_edges], 0.0)
        energy_row = jnp.sum(energy_weight * cell_speed * cell_speed, axis=0)
        ends = jnp.where(end_keep, energy_row[end_cells], 0.0)
        gradient_row = (ends[1] - ends[0]) * inverse_distance
        return flux_row - gradient_row, tangent_row, energy_row

    partial_sum, tangent, energy = lax.map(level_terms, (velocity, thickness, vorticity))
    zero_row = jnp.zeros_like(velocity[:1])
    above = jnp.concatenate([velocity[1:], zero_row], axis=0)
    below = jnp.concatenate([zero_row, velocity[:-1]], axis=0)
    advect = -0.5 * vertical_wind * (above - below)
    return partial_sum + advect, tangent, energy
```

```python
import functools

import jax
import jax.numpy as jnp
from jax import lax
from jax.experimental import pallas as pl
from jax.experimental.pallas import tpu as pltpu
from jax.sharding import PartitionSpec as P

MESH = pl.DeviceIdType.MESH
LANES = 128
SUB = 8
ALONG_LANES = lax.GatherDimensionNumbers(
    offset_dims=(),
    collapsed_slice_dims=(1,),
    start_index_map=(1,),
    operand_batching_dims=(0,),
    start_indices_batching_dims=(0,),
)


def pick(row, lanes):
    return lax.gather(
        row,
        lanes[..., None],
        ALONG_LANES,
        slice_sizes=(1, 1),
        mode=lax.GatherScatterMode.PROMISE_IN_BOUNDS,
    )


def tile(c):
    return pl.ds(pl.multiple_of(c * LANES, LANES), LANES)


def spread(row):
    return jnp.broadcast_to(row, (SUB, LANES))


def scan(first, last, load_rows, lookups, found, unroll):
    def step(k, found):
        rows = load_rows(k)
        after = []
        for (row_of, lane_of), held in zip(lookups, found):
            hit = row_of == k
            after.append(tuple(jnp.where(hit, pick(r, lane_of), h) for r, h in zip(rows, held)))
        return tuple(after)

    return lax.fori_loop(first, last, step, tuple(found), unroll=unroll)


def total_rows(x):
    return jnp.sum(x, axis=0, keepdims=True)


def kernel(
    n_mesh,
    n_lev,
    vel_h, thk_h, vor_h, wind_h, wts_h, eoe_h, eoc_h, coe_h, ew_h, invd_h, ehl_h, ehc_h, chl_h, chc_h,
    tend, tang, energy,
    vel, thk, vor, wind, wts, eoe, eoc, coe, ew, invd, ehl, ehc, chl, chc,
    below, above, esend, erecv, csend, crecv, near, cell_near, cell_pick,
    load_sem, es_sem, er_sem, cs_sem, cr_sem, ls_sem, lr_sem,
):
    levels, edges = vel.shape
    cells = energy.shape[1]
    blocks = ehl.shape[0]
    reach = blocks // 2
    halo_c = chl.shape[1]
    neoe, neoc = eoe.shape[0], eoc.shape[0]
    extra = neoe - SUB
    group = SUB // extra
    units = edges // (LANES * group)
    edge_rows = edges // LANES
    cell_rows = cells // LANES
    planes = 3 * levels
    me = lax.axis_index("mesh")
    lev = lax.axis_index("lev")

    def partner(o):
        offset = o + 1 if o < reach else reach - 1 - o
        return {"mesh": lax.rem(me + offset + n_mesh, n_mesh)}

    up = {"lev": lax.rem(lev + 1, n_lev)}
    down = {"lev": lax.rem(lev + n_lev - 1, n_lev)}

    barrier = pltpu.get_barrier_semaphore()
    for o in range(blocks):
        pl.semaphore_signal(barrier, inc=1, device_id=partner(o), device_id_type=MESH)
    pl.semaphore_signal(barrier, inc=1, device_id=up, device_id_type=MESH)
    pl.semaphore_signal(barrier, inc=1, device_id=down, device_id_type=MESH)

    pairs = [
        (ehl_h, ehl), (ehc_h, ehc), (vel_h, vel), (thk_h, thk), (vor_h, vor),
        (eoc_h, eoc), (eoe_h, eoe), (ew_h, ew), (wts_h, wts), (chl_h, chl), (chc_h, chc),
        (coe_h, coe), (invd_h, invd), (wind_h, wind),
    ]
    loads = []
    for i, (src, dst) in enumerate(pairs):
        copy = pltpu.make_async_copy(src, dst, load_sem.at[i])
        copy.start()
        loads.append(copy)
    esend[...] = jnp.zeros_like(esend)
    csend[...] = jnp.zeros_like(csend)
    cell_pick[...] = jnp.zeros_like(cell_pick)

    sublane = lax.broadcasted_iota(jnp.int32, (SUB, LANES), 0)
    lane = lax.broadcasted_iota(jnp.int32, (SUB, LANES), 1)
    blank = jnp.zeros((SUB, LANES), jnp.float32)

    def live(counts):
        most = jnp.zeros((SUB, LANES), jnp.int32)
        for o in range(blocks):
            most = jnp.where(sublane == o, counts[o], most)
        return lane < most

    def field_rows(k):
        return [
            spread(field[l : l + 1, tile(k)]) for field in (vel, thk, vor) for l in range(levels)
        ]

    def speed_rows(k):
        return [spread(vel[l : l + 1, tile(k)]) for l in range(levels)]

    def padded_rows(x):
        return jnp.concatenate([x, jnp.zeros((SUB - x.shape[0], LANES), x.dtype)], axis=0)

    for copy in loads[:5]:
        copy.wait()
    index = padded_rows(ehl[...])
    (packed,) = scan(
        0, edge_rows, field_rows, [(index >> 7, index & 127)], [(blank,) * planes], 4
    )
    alive = live(ehc)
    for p in range(planes):
        block = jnp.where(alive, packed[p], 0.0)
        for o in range(blocks):
            esend[SUB * o + p : SUB * o + p + 1, :] = block[o : o + 1]

    pl.semaphore_wait(barrier, blocks + 2)
    edge_copies = []
    for o in range(blocks):
        rows = pl.ds(SUB * o, SUB)
        copy = pltpu.make_async_remote_copy(
            src_ref=esend.at[rows],
            dst_ref=erecv.at[rows],
            send_sem=es_sem.at[o],
            recv_sem=er_sem.at[o],
            device_id=partner(o),
            device_id_type=MESH,
        )
        copy.start()
        edge_copies.append(copy)
    rim_copies = []
    for i, (dst, target) in enumerate(((below, up), (above, down))):
        copy = pltpu.make_async_remote_copy(
            src_ref=vel,
            dst_ref=dst,
            send_sem=ls_sem.at[i],
            recv_sem=lr_sem.at[i],
            device_id=target,
            device_id_type=MESH,
        )
        copy.start()
        rim_copies.append(copy)

    loads[5].wait()
    cell_lookups = []
    for c in range(cell_rows):
        index = padded_rows(eoc[:, c * LANES : (c + 1) * LANES])
        cell_lookups.append((index >> 7, index & 127))
    found = scan(
        0, edge_rows, speed_rows, cell_lookups, [(blank,) * levels] * cell_rows, 1
    )
    for c in range(cell_rows):
        for l in range(levels):
            cell_near[c * levels + l] = found[c][l]

    loads[6].wait()

    def unit_lookups(u):
        lookups = []
        for q in range(group):
            index = eoe[0:SUB, tile(u * group + q)]
            lookups.append((index >> 7, index & 127))
        index = jnp.concatenate(
            [eoe[SUB:neoe, tile(u * group + q)] for q in range(group)], axis=0
        )
        lookups.append((index >> 7, index & 127))
        return lookups

    def local_unit(u, carry):
        found = scan(
            0, edge_rows, field_rows, unit_lookups(u), [(blank,) * planes] * (group + 1), 2
        )
        for g in range(group + 1):
            for p in range(planes):
                near[u, g * planes + p] = found[g][p]
        return carry

    lax.fori_loop(0, units, local_unit, 0)

    for copy in edge_copies:
        copy.wait()
    loads[7].wait()

    def halo_rows(count):
        def load(k):
            start = pl.multiple_of(SUB * (k - edge_rows), SUB)
            rows = erecv[pl.ds(start, SUB), :]
            return [spread(rows[p : p + 1]) for p in range(count)]

        return load

    found = [
        tuple(cell_near[c * levels + l] for l in range(levels)) for c in range(cell_rows)
    ]
    found = scan(edge_rows, edge_rows + blocks, halo_rows(levels), cell_lookups, found, 1)
    for c in range(cell_rows):
        weight = padded_rows(ew[:, c * LANES : (c + 1) * LANES])
        energy[:, c * LANES : (c + 1) * LANES] = jnp.concatenate(
            [total_rows(weight * found[c][l] * found[c][l]) for l in range(levels)], axis=0
        )

    for copy in loads[9:11]:
        copy.wait()
    cell_pick[0:blocks, 0:halo_c] = chl[...]
    index = cell_pick[...]

    def energy_rows(k):
        return [spread(energy[l : l + 1, tile(k)]) for l in range(levels)]

    (packed,) = scan(
        0, cell_rows, energy_rows, [(index >> 7, index & 127)], [(blank,) * levels], cell_rows
    )
    alive = live(chc)
    for l in range(levels):
        block = jnp.where(alive, packed[l], 0.0)
        for o in range(blocks):
            csend[SUB * o + l : SUB * o + l + 1, :] = block[o : o + 1]
    cell_copies = []
    for o in range(blocks):
        rows = pl.ds(SUB * o, SUB)
        copy = pltpu.make_async_remote_copy(
            src_ref=csend.at[rows],
            dst_ref=crecv.at[rows],
            send_sem=cs_sem.at[o],
            recv_sem=cr_sem.at[o],
            device_id=partner(o),
            device_id_type=MESH,
        )
        copy.start()
        cell_copies.append(copy)

    loads[8].wait()

    def halo_unit(u, carry):
        found = [
            tuple(near[u, g * planes + p] for p in range(planes)) for g in range(group + 1)
        ]
        found = scan(
            edge_rows, edge_rows + blocks, halo_rows(planes), unit_lookups(u), found, 1
        )
        cols = [tile(u * group + q) for q in range(group)]
        few = jnp.concatenate([wts[SUB:neoe, c] for c in cols], axis=0)
        tangents = [[] for _ in cols]
        fluxes = [[] for _ in cols]
        for l in range(levels):
            own = [vor[l : l + 1, c] for c in cols]
            speed, height, potential = (found[group][f * levels + l] for f in range(3))
            own_few = jnp.concatenate(
                [jnp.broadcast_to(v, (extra, LANES)) for v in own], axis=0
            )
            moved_few = few * speed
            flux_few = moved_few * height * 0.5 * (own_few + potential)
            for q, c in enumerate(cols):
                speed, height, potential = (found[q][f * levels + l] for f in range(3))
                moved = wts[0:SUB, c] * speed
                flux = moved * height * 0.5 * (spread(own[q]) + potential)
                part = slice(extra * q, extra * (q + 1))
                tangents[q].append(total_rows(moved) + total_rows(moved_few[part]))
                fluxes[q].append(total_rows(flux) + total_rows(flux_few[part]))
        for q, c in enumerate(cols):
            tang[:, c] = jnp.concatenate(tangents[q], axis=0)
            tend[:, c] = jnp.concatenate(fluxes[q], axis=0)
        return carry

    lax.fori_loop(0, units, halo_unit, 0)

    for copy in cell_copies + rim_copies + loads[11:]:
        copy.wait()
    ends = SUB // 2

    def end_unit(u, carry):
        cols = [tile(u * ends + q) for q in range(ends)]
        index = jnp.concatenate([coe[:, c] for c in cols], axis=0)
        far = index >= cells
        slot = index - cells
        place = (
            jnp.where(far, cell_rows + slot // halo_c, index >> 7),
            jnp.where(far, slot % halo_c, index & 127),
        )

        def received_rows(k):
            start = pl.multiple_of(SUB * (k - cell_rows), SUB)
            rows = crecv[pl.ds(start, SUB), :]
            return [spread(rows[l : l + 1]) for l in range(levels)]

        found = scan(0, cell_rows, energy_rows, [place], [(blank,) * levels], cell_rows)
        (found,) = scan(cell_rows, cell_rows + blocks, received_rows, [place], found, blocks)
        for q, c in enumerate(cols):
            rows = []
            for l in range(levels):
                gradient = (
                    found[l][2 * q + 1 : 2 * q + 2] - found[l][2 * q : 2 * q + 1]
                ) * invd[pl.ds(u * ends + q, 1), :]
                if l + 1 < levels:
                    over = vel[l + 1 : l + 2, c]
                else:
                    over = jnp.where(lev == n_lev - 1, 0.0, above[0:1, c])
                if l > 0:
                    under = vel[l - 1 : l, c]
                else:
                    under = jnp.where(lev == 0, 0.0, below[levels - 1 : levels, c])
                advect = -0.5 * wind[l : l + 1, c] * (over - under)
                rows.append((tend[l : l + 1, c] - gradient) + advect)
            tend[:, c] = jnp.concatenate(rows, axis=0)
        return carry

    lax.fori_loop(0, edge_rows // ends, end_unit, 0)


def body(
    velocity,
    thickness,
    vorticity,
    vertical_wind,
    weights_on_edge,
    edges_on_edge,
    edges_on_cell,
    cells_on_edge,
    energy_weight,
    inverse_distance,
    edge_halo_list,
    edge_halo_count,
    cell_halo_list,
    cell_halo_count,
):
    levels, edges = velocity.shape
    cells = edges_on_cell.shape[1]
    blocks = edge_halo_list.shape[0]
    group = SUB // (edges_on_edge.shape[0] - SUB)
    units = edges // (LANES * group)
    args = [
        velocity, thickness, vorticity, vertical_wind, weights_on_edge, edges_on_edge,
        edges_on_cell, cells_on_edge, energy_weight, inverse_distance.reshape(-1, LANES),
        edge_halo_list, edge_halo_count, cell_halo_list, cell_halo_count,
    ]
    held = [
        pltpu.SMEM(a.shape, a.dtype) if a.ndim == 1 else pltpu.VMEM(a.shape, a.dtype) for a in args
    ]
    exchange = pltpu.VMEM((SUB * blocks, LANES), jnp.float32)
    dma = lambda n: pltpu.SemaphoreType.DMA((n,))
    return pl.pallas_call(
        functools.partial(kernel, lax.axis_size("mesh"), lax.axis_size("lev")),
        out_shape=(
            jax.ShapeDtypeStruct((levels, edges), jnp.float32),
            jax.ShapeDtypeStruct((levels, edges), jnp.float32),
            jax.ShapeDtypeStruct((levels, cells), jnp.float32),
        ),
        in_specs=[pl.BlockSpec(memory_space=pl.ANY)] * len(args),
        out_specs=(pl.BlockSpec(memory_space=pltpu.VMEM),) * 3,
        scratch_shapes=held
        + [
            pltpu.VMEM((levels, edges), jnp.float32),
            pltpu.VMEM((levels, edges), jnp.float32),
            exchange, exchange, exchange, exchange,
            pltpu.VMEM((units, (group + 1) * 3 * levels, SUB, LANES), jnp.float32),
            pltpu.VMEM((cells // LANES * levels, SUB, LANES), jnp.float32),
            pltpu.VMEM((SUB, LANES), jnp.int32),
            dma(len(args)), dma(blocks), dma(blocks), dma(blocks), dma(blocks), dma(2), dma(2),
        ],
        compiler_params=pltpu.CompilerParams(collective_id=0, has_side_effects=True),
    )(*args)


def solution(mesh):
    in_specs = (
        P("lev", "mesh"),
        P("lev", "mesh"),
        P("lev", "mesh"),
        P("lev", "mesh"),
        P(None, "mesh"),
        P(None, "mesh"),
        P(None, "mesh"),
        P(None, "mesh"),
        P(None, "mesh"),
        P("mesh"),
        P("mesh", None),
        P("mesh"),
        P("mesh", None),
        P("mesh"),
    )
    out_specs = (P("lev", "mesh"), P("lev", "mesh"), P("lev", "mesh"))
    return jax.shard_map(body, mesh=mesh, in_specs=in_specs, out_specs=out_specs, check_vma=False)
```

```python
import functools

import jax
import jax.numpy as jnp
from jax import lax
from jax.experimental import pallas as pl
from jax.experimental.pallas import tpu as pltpu
from jax.sharding import PartitionSpec as P

MESH = pl.DeviceIdType.MESH
LANES = 128
SUB = 8
ALONG_LANES = lax.GatherDimensionNumbers(
    offset_dims=(),
    collapsed_slice_dims=(1,),
    start_index_map=(1,),
    operand_batching_dims=(0,),
    start_indices_batching_dims=(0,),
)


def pick(row, lanes):
    return lax.gather(
        row,
        lanes[..., None],
        ALONG_LANES,
        slice_sizes=(1, 1),
        mode=lax.GatherScatterMode.PROMISE_IN_BOUNDS,
    )


def tile(c):
    return pl.ds(pl.multiple_of(c * LANES, LANES), LANES)


def spread(row):
    return jnp.broadcast_to(row, (SUB, LANES))


def scan(first, last, load_rows, lookups, found, unroll):
    def step(k, found):
        rows = load_rows(k)
        after = []
        for (row_of, lane_of), held in zip(lookups, found):
            hit = row_of == k
            after.append(tuple(jnp.where(hit, pick(r, lane_of), h) for r, h in zip(rows, held)))
        return tuple(after)

    return lax.fori_loop(first, last, step, tuple(found), unroll=unroll)


def total_rows(x):
    return jnp.sum(x, axis=0, keepdims=True)


def kernel(
    n_mesh,
    n_lev,
    vel_h, thk_h, vor_h, wind_h, wts_h, eoe_h, eoc_h, coe_h, ew_h, invd_h, ehl_h, ehc_h, chl_h, chc_h,
    tend, tang, energy,
    vel, thk, vor, wind, wts, eoe, eoc, coe, ew, invd, ehl, ehc, chl, chc,
    below, above, esend, erecv, csend, crecv, near, cell_near, cell_pick,
    load_sem, es_sem, er_sem, cs_sem, cr_sem, ls_sem, lr_sem,
):
    levels, edges = vel.shape
    cells = energy.shape[1]
    blocks = ehl.shape[0]
    reach = blocks // 2
    halo_c = chl.shape[1]
    neoe, neoc = eoe.shape[0], eoc.shape[0]
    extra = neoe - SUB
    group = SUB // extra
    units = edges // (LANES * group)
    edge_rows = edges // LANES
    cell_rows = cells // LANES
    planes = 3 * levels
    me = lax.axis_index("mesh")
    lev = lax.axis_index("lev")

    def partner(o):
        offset = o + 1 if o < reach else reach - 1 - o
        return {"mesh": lax.rem(me + offset + n_mesh, n_mesh)}

    up = {"lev": lax.rem(lev + 1, n_lev)}
    down = {"lev": lax.rem(lev + n_lev - 1, n_lev)}

    barrier = pltpu.get_barrier_semaphore()
    for o in range(blocks):
        pl.semaphore_signal(barrier, inc=1, device_id=partner(o), device_id_type=MESH)
    pl.semaphore_signal(barrier, inc=1, device_id=up, device_id_type=MESH)
    pl.semaphore_signal(barrier, inc=1, device_id=down, device_id_type=MESH)

    pairs = [
        (ehl_h, ehl), (ehc_h, ehc), (vel_h, vel), (thk_h, thk), (vor_h, vor),
        (eoc_h, eoc), (eoe_h, eoe), (ew_h, ew), (wts_h, wts), (chl_h, chl), (chc_h, chc),
        (coe_h, coe), (invd_h, invd), (wind_h, wind),
    ]
    loads = []
    for i, (src, dst) in enumerate(pairs):
        copy = pltpu.make_async_copy(src, dst, load_sem.at[i])
        copy.start()
        loads.append(copy)
    esend[...] = jnp.zeros_like(esend)
    csend[...] = jnp.zeros_like(csend)
    cell_pick[...] = jnp.zeros_like(cell_pick)

    sublane = lax.broadcasted_iota(jnp.int32, (SUB, LANES), 0)
    lane = lax.broadcasted_iota(jnp.int32, (SUB, LANES), 1)
    blank = jnp.zeros((SUB, LANES), jnp.float32)

    def live(counts):
        most = jnp.zeros((SUB, LANES), jnp.int32)
        for o in range(blocks):
            most = jnp.where(sublane == o, counts[o], most)
        return lane < most

    def field_rows(k):
        return [
            spread(field[l : l + 1, tile(k)]) for field in (vel, thk, vor) for l in range(levels)
        ]

    def speed_rows(k):
        return [spread(vel[l : l + 1, tile(k)]) for l in range(levels)]

    def padded_rows(x):
        return jnp.concatenate([x, jnp.zeros((SUB - x.shape[0], LANES), x.dtype)], axis=0)

    for copy in loads[:5]:
        copy.wait()
    index = padded_rows(ehl[...])
    (packed,) = scan(
        0, edge_rows, field_rows, [(index >> 7, index & 127)], [(blank,) * planes], edge_rows
    )
    alive = live(ehc)
    for p in range(planes):
        block = jnp.where(alive, packed[p], 0.0)
        for o in range(blocks):
            esend[SUB * o + p : SUB * o + p + 1, :] = block[o : o + 1]

    pl.semaphore_wait(barrier, blocks + 2)
    edge_copies = []
    for o in range(blocks):
        rows = pl.ds(SUB * o, SUB)
        copy = pltpu.make_async_remote_copy(
            src_ref=esend.at[rows],
            dst_ref=erecv.at[rows],
            send_sem=es_sem.at[o],
            recv_sem=er_sem.at[o],
            device_id=partner(o),
            device_id_type=MESH,
        )
        copy.start()
        edge_copies.append(copy)
    rim_copies = []
    for i, (dst, target) in enumerate(((below, up), (above, down))):
        copy = pltpu.make_async_remote_copy(
            src_ref=vel,
            dst_ref=dst,
            send_sem=ls_sem.at[i],
            recv_sem=lr_sem.at[i],
            device_id=target,
            device_id_type=MESH,
        )
        copy.start()
        rim_copies.append(copy)

    loads[5].wait()
    cell_lookups = []
    for c in range(cell_rows):
        index = padded_rows(eoc[:, c * LANES : (c + 1) * LANES])
        cell_lookups.append((index >> 7, index & 127))
    found = scan(
        0, edge_rows, speed_rows, cell_lookups, [(blank,) * levels] * cell_rows, edge_rows
    )
    for c in range(cell_rows):
        for l in range(levels):
            cell_near[c * levels + l] = found[c][l]

    loads[6].wait()

    def unit_lookups(u):
        lookups = []
        for q in range(group):
            index = eoe[0:SUB, tile(u * group + q)]
            lookups.append((index >> 7, index & 127))
        index = jnp.concatenate(
            [eoe[SUB:neoe, tile(u * group + q)] for q in range(group)], axis=0
        )
        lookups.append((index >> 7, index & 127))
        return lookups

    def local_unit(u, carry):
        found = scan(
            0, edge_rows, field_rows, unit_lookups(u), [(blank,) * planes] * (group + 1), edge_rows
        )
        for g in range(group + 1):
            for p in range(planes):
                near[u, g * planes + p] = found[g][p]
        return carry

    lax.fori_loop(0, units, local_unit, 0)

    for copy in edge_copies:
        copy.wait()
    loads[7].wait()

    def halo_rows(count):
        def load(k):
            start = pl.multiple_of(SUB * (k - edge_rows), SUB)
            rows = erecv[pl.ds(start, SUB), :]
            return [spread(rows[p : p + 1]) for p in range(count)]

        return load

    found = [
        tuple(cell_near[c * levels + l] for l in range(levels)) for c in range(cell_rows)
    ]
    found = scan(edge_rows, edge_rows + blocks, halo_rows(levels), cell_lookups, found, blocks)
    for c in range(cell_rows):
        weight = padded_rows(ew[:, c * LANES : (c + 1) * LANES])
        energy[:, c * LANES : (c + 1) * LANES] = jnp.concatenate(
            [total_rows(weight * found[c][l] * found[c][l]) for l in range(levels)], axis=0
        )

    for copy in loads[9:11]:
        copy.wait()
    cell_pick[0:blocks, 0:halo_c] = chl[...]
    index = cell_pick[...]

    def energy_rows(k):
        return [spread(energy[l : l + 1, tile(k)]) for l in range(levels)]

    (packed,) = scan(
        0, cell_rows, energy_rows, [(index >> 7, index & 127)], [(blank,) * levels], cell_rows
    )
    alive = live(chc)
    for l in range(levels):
        block = jnp.where(alive, packed[l], 0.0)
        for o in range(blocks):
            csend[SUB * o + l : SUB * o + l + 1, :] = block[o : o + 1]
    cell_copies = []
    for o in range(blocks):
        rows = pl.ds(SUB * o, SUB)
        copy = pltpu.make_async_remote_copy(
            src_ref=csend.at[rows],
            dst_ref=crecv.at[rows],
            send_sem=cs_sem.at[o],
            recv_sem=cr_sem.at[o],
            device_id=partner(o),
            device_id_type=MESH,
        )
        copy.start()
        cell_copies.append(copy)

    loads[8].wait()

    def halo_unit(u, carry):
        found = [
            tuple(near[u, g * planes + p] for p in range(planes)) for g in range(group + 1)
        ]
        found = scan(
            edge_rows, edge_rows + blocks, halo_rows(planes), unit_lookups(u), found, blocks
        )
        cols = [tile(u * group + q) for q in range(group)]
        few = jnp.concatenate([wts[SUB:neoe, c] for c in cols], axis=0)
        tangents = [[] for _ in cols]
        fluxes = [[] for _ in cols]
        for l in range(levels):
            own = [vor[l : l + 1, c] for c in cols]
            speed, height, potential = (found[group][f * levels + l] for f in range(3))
            own_few = jnp.concatenate(
                [jnp.broadcast_to(v, (extra, LANES)) for v in own], axis=0
            )
            moved_few = few * speed
            flux_few = moved_few * height * 0.5 * (own_few + potential)
            for q, c in enumerate(cols):
                speed, height, potential = (found[q][f * levels + l] for f in range(3))
                moved = wts[0:SUB, c] * speed
                flux = moved * height * 0.5 * (spread(own[q]) + potential)
                part = slice(extra * q, extra * (q + 1))
                tangents[q].append(total_rows(moved) + total_rows(moved_few[part]))
                fluxes[q].append(total_rows(flux) + total_rows(flux_few[part]))
        for q, c in enumerate(cols):
            tang[:, c] = jnp.concatenate(tangents[q], axis=0)
            tend[:, c] = jnp.concatenate(fluxes[q], axis=0)
        return carry

    lax.fori_loop(0, units, halo_unit, 0)

    for copy in cell_copies + rim_copies + loads[11:]:
        copy.wait()
    ends = SUB // 2

    def end_unit(u, carry):
        cols = [tile(u * ends + q) for q in range(ends)]
        index = jnp.concatenate([coe[:, c] for c in cols], axis=0)
        far = index >= cells
        slot = index - cells
        place = (
            jnp.where(far, cell_rows + slot // halo_c, index >> 7),
            jnp.where(far, slot % halo_c, index & 127),
        )

        def received_rows(k):
            start = pl.multiple_of(SUB * (k - cell_rows), SUB)
            rows = crecv[pl.ds(start, SUB), :]
            return [spread(rows[l : l + 1]) for l in range(levels)]

        found = scan(0, cell_rows, energy_rows, [place], [(blank,) * levels], cell_rows)
        (found,) = scan(cell_rows, cell_rows + blocks, received_rows, [place], found, blocks)
        for q, c in enumerate(cols):
            rows = []
            for l in range(levels):
                gradient = (
                    found[l][2 * q + 1 : 2 * q + 2] - found[l][2 * q : 2 * q + 1]
                ) * invd[pl.ds(u * ends + q, 1), :]
                if l + 1 < levels:
                    over = vel[l + 1 : l + 2, c]
                else:
                    over = jnp.where(lev == n_lev - 1, 0.0, above[0:1, c])
                if l > 0:
                    under = vel[l - 1 : l, c]
                else:
                    under = jnp.where(lev == 0, 0.0, below[levels - 1 : levels, c])
                advect = -0.5 * wind[l : l + 1, c] * (over - under)
                rows.append((tend[l : l + 1, c] - gradient) + advect)
            tend[:, c] = jnp.concatenate(rows, axis=0)
        return carry

    lax.fori_loop(0, edge_rows // ends, end_unit, 0)


def body(
    velocity,
    thickness,
    vorticity,
    vertical_wind,
    weights_on_edge,
    edges_on_edge,
    edges_on_cell,
    cells_on_edge,
    energy_weight,
    inverse_distance,
    edge_halo_list,
    edge_halo_count,
    cell_halo_list,
    cell_halo_count,
):
    levels, edges = velocity.shape
    cells = edges_on_cell.shape[1]
    blocks = edge_halo_list.shape[0]
    group = SUB // (edges_on_edge.shape[0] - SUB)
    units = edges // (LANES * group)
    args = [
        velocity, thickness, vorticity, vertical_wind, weights_on_edge, edges_on_edge,
        edges_on_cell, cells_on_edge, energy_weight, inverse_distance.reshape(-1, LANES),
        edge_halo_list, edge_halo_count, cell_halo_list, cell_halo_count,
    ]
    held = [
        pltpu.SMEM(a.shape, a.dtype) if a.ndim == 1 else pltpu.VMEM(a.shape, a.dtype) for a in args
    ]
    exchange = pltpu.VMEM((SUB * blocks, LANES), jnp.float32)
    dma = lambda n: pltpu.SemaphoreType.DMA((n,))
    return pl.pallas_call(
        functools.partial(kernel, lax.axis_size("mesh"), lax.axis_size("lev")),
        out_shape=(
            jax.ShapeDtypeStruct((levels, edges), jnp.float32),
            jax.ShapeDtypeStruct((levels, edges), jnp.float32),
            jax.ShapeDtypeStruct((levels, cells), jnp.float32),
        ),
        in_specs=[pl.BlockSpec(memory_space=pl.ANY)] * len(args),
        out_specs=(pl.BlockSpec(memory_space=pltpu.VMEM),) * 3,
        scratch_shapes=held
        + [
            pltpu.VMEM((levels, edges), jnp.float32),
            pltpu.VMEM((levels, edges), jnp.float32),
            exchange, exchange, exchange, exchange,
            pltpu.VMEM((units, (group + 1) * 3 * levels, SUB, LANES), jnp.float32),
            pltpu.VMEM((cells // LANES * levels, SUB, LANES), jnp.float32),
            pltpu.VMEM((SUB, LANES), jnp.int32),
            dma(len(args)), dma(blocks), dma(blocks), dma(blocks), dma(blocks), dma(2), dma(2),
        ],
        compiler_params=pltpu.CompilerParams(collective_id=0, has_side_effects=True),
    )(*args)


def solution(mesh):
    in_specs = (
        P("lev", "mesh"),
        P("lev", "mesh"),
        P("lev", "mesh"),
        P("lev", "mesh"),
        P(None, "mesh"),
        P(None, "mesh"),
        P(None, "mesh"),
        P(None, "mesh"),
        P(None, "mesh"),
        P("mesh"),
        P("mesh", None),
        P("mesh"),
        P("mesh", None),
        P("mesh"),
    )
    out_specs = (P("lev", "mesh"), P("lev", "mesh"), P("lev", "mesh"))
    return jax.shard_map(body, mesh=mesh, in_specs=in_specs, out_specs=out_specs, check_vma=False)
```

```python
import functools

import jax
import jax.numpy as jnp
from jax import lax
from jax.experimental import pallas as pl
from jax.experimental.pallas import tpu as pltpu
from jax.sharding import PartitionSpec as P

MESH = pl.DeviceIdType.MESH
LANES = 128
SUB = 8
ALONG_LANES = lax.GatherDimensionNumbers(
    offset_dims=(),
    collapsed_slice_dims=(1,),
    start_index_map=(1,),
    operand_batching_dims=(0,),
    start_indices_batching_dims=(0,),
)


def pick(row, lanes):
    return lax.gather(
        row,
        lanes[..., None],
        ALONG_LANES,
        slice_sizes=(1, 1),
        mode=lax.GatherScatterMode.PROMISE_IN_BOUNDS,
    )


def tile(c):
    return pl.ds(pl.multiple_of(c * LANES, LANES), LANES)


def spread(row):
    return jnp.broadcast_to(row, (SUB, LANES))


def scan(first, last, load_rows, lookups, found, unroll):
    def step(k, found):
        rows = load_rows(k)
        after = []
        for (row_of, lane_of), held in zip(lookups, found):
            hit = row_of == k
            after.append(tuple(jnp.where(hit, pick(r, lane_of), h) for r, h in zip(rows, held)))
        return tuple(after)

    return lax.fori_loop(first, last, step, tuple(found), unroll=unroll)


def total_rows(x):
    return jnp.sum(x, axis=0, keepdims=True)


def kernel(
    n_mesh,
    n_lev,
    vel_h, thk_h, vor_h, wind_h, wts_h, eoe_h, eoc_h, coe_h, ew_h, invd_h, ehl_h, ehc_h, chl_h, chc_h,
    tend_h, tang_h, energy_h,
    vel, thk, vor, wind, wts, eoe, eoc, coe, ew, invd, ehl, ehc, chl, chc,
    tend, tang, energy, below, above, esend, erecv, csend, crecv, near, cell_near, cell_pick,
    load_sem, es_sem, er_sem, cs_sem, cr_sem, ls_sem, lr_sem, out_sem,
):
    levels, edges = vel.shape
    cells = energy.shape[1]
    blocks = ehl.shape[0]
    reach = blocks // 2
    halo_c = chl.shape[1]
    neoe, neoc = eoe.shape[0], eoc.shape[0]
    extra = neoe - SUB
    group = SUB // extra
    units = edges // (LANES * group)
    edge_rows = edges // LANES
    cell_rows = cells // LANES
    planes = 3 * levels
    me = lax.axis_index("mesh")
    lev = lax.axis_index("lev")

    def partner(o):
        offset = o + 1 if o < reach else reach - 1 - o
        return {"mesh": lax.rem(me + offset + n_mesh, n_mesh)}

    up = {"lev": lax.rem(lev + 1, n_lev)}
    down = {"lev": lax.rem(lev + n_lev - 1, n_lev)}

    barrier = pltpu.get_barrier_semaphore()
    for o in range(blocks):
        pl.semaphore_signal(barrier, inc=1, device_id=partner(o), device_id_type=MESH)
    pl.semaphore_signal(barrier, inc=1, device_id=up, device_id_type=MESH)
    pl.semaphore_signal(barrier, inc=1, device_id=down, device_id_type=MESH)

    pairs = [
        (ehl_h, ehl), (ehc_h, ehc), (vel_h, vel), (thk_h, thk), (vor_h, vor),
        (eoc_h, eoc), (eoe_h, eoe), (ew_h, ew), (wts_h, wts), (chl_h, chl), (chc_h, chc),
        (coe_h, coe), (invd_h, invd), (wind_h, wind),
    ]
    loads = []
    for i, (src, dst) in enumerate(pairs):
        copy = pltpu.make_async_copy(src, dst, load_sem.at[i])
        copy.start()
        loads.append(copy)
    esend[...] = jnp.zeros_like(esend)
    csend[...] = jnp.zeros_like(csend)
    cell_pick[...] = jnp.zeros_like(cell_pick)

    sublane = lax.broadcasted_iota(jnp.int32, (SUB, LANES), 0)
    lane = lax.broadcasted_iota(jnp.int32, (SUB, LANES), 1)
    blank = jnp.zeros((SUB, LANES), jnp.float32)

    def live(counts):
        most = jnp.zeros((SUB, LANES), jnp.int32)
        for o in range(blocks):
            most = jnp.where(sublane == o, counts[o], most)
        return lane < most

    def field_rows(k):
        return [
            spread(field[l : l + 1, tile(k)]) for field in (vel, thk, vor) for l in range(levels)
        ]

    def speed_rows(k):
        return [spread(vel[l : l + 1, tile(k)]) for l in range(levels)]

    def padded_rows(x):
        return jnp.concatenate([x, jnp.zeros((SUB - x.shape[0], LANES), x.dtype)], axis=0)

    for copy in loads[:5]:
        copy.wait()
    index = padded_rows(ehl[...])
    (packed,) = scan(
        0, edge_rows, field_rows, [(index >> 7, index & 127)], [(blank,) * planes], edge_rows
    )
    alive = live(ehc)
    for p in range(planes):
        block = jnp.where(alive, packed[p], 0.0)
        for o in range(blocks):
            esend[SUB * o + p : SUB * o + p + 1, :] = block[o : o + 1]

    pl.semaphore_wait(barrier, blocks + 2)
    edge_copies = []
    for o in range(blocks):
        rows = pl.ds(SUB * o, SUB)
        copy = pltpu.make_async_remote_copy(
            src_ref=esend.at[rows],
            dst_ref=erecv.at[rows],
            send_sem=es_sem.at[o],
            recv_sem=er_sem.at[o],
            device_id=partner(o),
            device_id_type=MESH,
        )
        copy.start()
        edge_copies.append(copy)
    rim_copies = []
    for i, (dst, target) in enumerate(((below, up), (above, down))):
        copy = pltpu.make_async_remote_copy(
            src_ref=vel,
            dst_ref=dst,
            send_sem=ls_sem.at[i],
            recv_sem=lr_sem.at[i],
            device_id=target,
            device_id_type=MESH,
        )
        copy.start()
        rim_copies.append(copy)

    loads[5].wait()
    cell_lookups = []
    for c in range(cell_rows):
        index = padded_rows(eoc[:, c * LANES : (c + 1) * LANES])
        cell_lookups.append((index >> 7, index & 127))
    found = scan(
        0, edge_rows, speed_rows, cell_lookups, [(blank,) * levels] * cell_rows, edge_rows
    )
    for c in range(cell_rows):
        for l in range(levels):
            cell_near[c * levels + l] = found[c][l]

    loads[6].wait()

    def unit_lookups(u):
        lookups = []
        for q in range(group):
            index = eoe[0:SUB, tile(u * group + q)]
            lookups.append((index >> 7, index & 127))
        index = jnp.concatenate(
            [eoe[SUB:neoe, tile(u * group + q)] for q in range(group)], axis=0
        )
        lookups.append((index >> 7, index & 127))
        return lookups

    def local_unit(u, carry):
        found = scan(
            0, edge_rows, field_rows, unit_lookups(u), [(blank,) * planes] * (group + 1), edge_rows
        )
        for g in range(group + 1):
            for p in range(planes):
                near[u, g * planes + p] = found[g][p]
        return carry

    lax.fori_loop(0, units, local_unit, 0)

    for copy in edge_copies:
        copy.wait()
    loads[7].wait()

    def halo_rows(count):
        def load(k):
            start = pl.multiple_of(SUB * (k - edge_rows), SUB)
            rows = erecv[pl.ds(start, SUB), :]
            return [spread(rows[p : p + 1]) for p in range(count)]

        return load

    found = [
        tuple(cell_near[c * levels + l] for l in range(levels)) for c in range(cell_rows)
    ]
    found = scan(edge_rows, edge_rows + blocks, halo_rows(levels), cell_lookups, found, blocks)
    for c in range(cell_rows):
        weight = padded_rows(ew[:, c * LANES : (c + 1) * LANES])
        energy[:, c * LANES : (c + 1) * LANES] = jnp.concatenate(
            [total_rows(weight * found[c][l] * found[c][l]) for l in range(levels)], axis=0
        )

    energy_out = pltpu.make_async_copy(energy, energy_h, out_sem.at[0])
    energy_out.start()

    for copy in loads[9:11]:
        copy.wait()
    cell_pick[0:blocks, 0:halo_c] = chl[...]
    index = cell_pick[...]

    def energy_rows(k):
        return [spread(energy[l : l + 1, tile(k)]) for l in range(levels)]

    (packed,) = scan(
        0, cell_rows, energy_rows, [(index >> 7, index & 127)], [(blank,) * levels], cell_rows
    )
    alive = live(chc)
    for l in range(levels):
        block = jnp.where(alive, packed[l], 0.0)
        for o in range(blocks):
            csend[SUB * o + l : SUB * o + l + 1, :] = block[o : o + 1]
    cell_copies = []
    for o in range(blocks):
        rows = pl.ds(SUB * o, SUB)
        copy = pltpu.make_async_remote_copy(
            src_ref=csend.at[rows],
            dst_ref=crecv.at[rows],
            send_sem=cs_sem.at[o],
            recv_sem=cr_sem.at[o],
            device_id=partner(o),
            device_id_type=MESH,
        )
        copy.start()
        cell_copies.append(copy)

    loads[8].wait()

    def halo_unit(u, carry):
        found = [
            tuple(near[u, g * planes + p] for p in range(planes)) for g in range(group + 1)
        ]
        found = scan(
            edge_rows, edge_rows + blocks, halo_rows(planes), unit_lookups(u), found, blocks
        )
        cols = [tile(u * group + q) for q in range(group)]
        few = jnp.concatenate([wts[SUB:neoe, c] for c in cols], axis=0)
        tangents = [[] for _ in cols]
        fluxes = [[] for _ in cols]
        for l in range(levels):
            own = [vor[l : l + 1, c] for c in cols]
            speed, height, potential = (found[group][f * levels + l] for f in range(3))
            own_few = jnp.concatenate(
                [jnp.broadcast_to(v, (extra, LANES)) for v in own], axis=0
            )
            moved_few = few * speed
            flux_few = moved_few * height * 0.5 * (own_few + potential)
            for q, c in enumerate(cols):
                speed, height, potential = (found[q][f * levels + l] for f in range(3))
                moved = wts[0:SUB, c] * speed
                flux = moved * height * 0.5 * (spread(own[q]) + potential)
                part = slice(extra * q, extra * (q + 1))
                tangents[q].append(total_rows(moved) + total_rows(moved_few[part]))
                fluxes[q].append(total_rows(flux) + total_rows(flux_few[part]))
        for q, c in enumerate(cols):
            tang[:, c] = jnp.concatenate(tangents[q], axis=0)
            tend[:, c] = jnp.concatenate(fluxes[q], axis=0)
        return carry

    lax.fori_loop(0, units, halo_unit, 0, unroll=2)
    tang_out = pltpu.make_async_copy(tang, tang_h, out_sem.at[1])
    tang_out.start()

    for copy in cell_copies + rim_copies + loads[11:]:
        copy.wait()
    ends = SUB // 2

    def end_unit(u, carry):
        cols = [tile(u * ends + q) for q in range(ends)]
        index = jnp.concatenate([coe[:, c] for c in cols], axis=0)
        far = index >= cells
        slot = index - cells
        place = (
            jnp.where(far, cell_rows + slot // halo_c, index >> 7),
            jnp.where(far, slot % halo_c, index & 127),
        )

        def received_rows(k):
            start = pl.multiple_of(SUB * (k - cell_rows), SUB)
            rows = crecv[pl.ds(start, SUB), :]
            return [spread(rows[l : l + 1]) for l in range(levels)]

        found = scan(0, cell_rows, energy_rows, [place], [(blank,) * levels], cell_rows)
        (found,) = scan(cell_rows, cell_rows + blocks, received_rows, [place], found, blocks)
        for q, c in enumerate(cols):
            rows = []
            for l in range(levels):
                gradient = (
                    found[l][2 * q + 1 : 2 * q + 2] - found[l][2 * q : 2 * q + 1]
                ) * invd[pl.ds(u * ends + q, 1), :]
                if l + 1 < levels:
                    over = vel[l + 1 : l + 2, c]
                else:
                    over = jnp.where(lev == n_lev - 1, 0.0, above[0:1, c])
                if l > 0:
                    under = vel[l - 1 : l, c]
                else:
                    under = jnp.where(lev == 0, 0.0, below[levels - 1 : levels, c])
                advect = -0.5 * wind[l : l + 1, c] * (over - under)
                rows.append((tend[l : l + 1, c] - gradient) + advect)
            tend[:, c] = jnp.concatenate(rows, axis=0)
        return carry

    lax.fori_loop(0, edge_rows // ends, end_unit, 0, unroll=edge_rows // ends)
    tend_out = pltpu.make_async_copy(tend, tend_h, out_sem.at[2])
    tend_out.start()
    for copy in (energy_out, tang_out, tend_out):
        copy.wait()


def place(*refs):
    *pairs, sem = refs
    half = len(pairs) // 2
    copies = [
        pltpu.make_async_copy(pairs[i], pairs[half + i], sem.at[i]) for i in range(half)
    ]
    for copy in copies:
        copy.start()
    for copy in copies:
        copy.wait()


def body(
    velocity,
    thickness,
    vorticity,
    vertical_wind,
    weights_on_edge,
    edges_on_edge,
    edges_on_cell,
    cells_on_edge,
    energy_weight,
    inverse_distance,
    edge_halo_list,
    edge_halo_count,
    cell_halo_list,
    cell_halo_count,
):
    levels, edges = velocity.shape
    cells = edges_on_cell.shape[1]
    blocks = edge_halo_list.shape[0]
    group = SUB // (edges_on_edge.shape[0] - SUB)
    units = edges // (LANES * group)
    args = [
        velocity, thickness, vorticity, vertical_wind, weights_on_edge, edges_on_edge,
        edges_on_cell, cells_on_edge, energy_weight, inverse_distance.reshape(-1, LANES),
        edge_halo_list, edge_halo_count, cell_halo_list, cell_halo_count,
    ]
    held = [
        pltpu.SMEM(a.shape, a.dtype) if a.ndim == 1 else pltpu.VMEM(a.shape, a.dtype) for a in args
    ]
    exchange = pltpu.VMEM((SUB * blocks, LANES), jnp.float32)
    dma = lambda n: pltpu.SemaphoreType.DMA((n,))
    results = (
        jax.ShapeDtypeStruct((levels, edges), jnp.float32),
        jax.ShapeDtypeStruct((levels, edges), jnp.float32),
        jax.ShapeDtypeStruct((levels, cells), jnp.float32),
    )
    anywhere = pl.BlockSpec(memory_space=pl.ANY)
    found = pl.pallas_call(
        functools.partial(kernel, lax.axis_size("mesh"), lax.axis_size("lev")),
        out_shape=results,
        in_specs=[anywhere] * len(args),
        out_specs=(anywhere,) * 3,
        scratch_shapes=held
        + [
            pltpu.VMEM((levels, edges), jnp.float32),
            pltpu.VMEM((levels, edges), jnp.float32),
            pltpu.VMEM((levels, cells), jnp.float32),
            pltpu.VMEM((levels, edges), jnp.float32),
            pltpu.VMEM((levels, edges), jnp.float32),
            exchange, exchange, exchange, exchange,
            pltpu.VMEM((units, (group + 1) * 3 * levels, SUB, LANES), jnp.float32),
            pltpu.VMEM((cells // LANES * levels, SUB, LANES), jnp.float32),
            pltpu.VMEM((SUB, LANES), jnp.int32),
            dma(len(args)), dma(blocks), dma(blocks), dma(blocks), dma(blocks), dma(2), dma(2), dma(3),
        ],
        compiler_params=pltpu.CompilerParams(collective_id=0, has_side_effects=True),
    )(*args)
    return pl.pallas_call(
        place,
        out_shape=results,
        in_specs=[anywhere] * 3,
        out_specs=(anywhere,) * 3,
        scratch_shapes=[dma(3)],
    )(*found)


def solution(mesh):
    in_specs = (
        P("lev", "mesh"),
        P("lev", "mesh"),
        P("lev", "mesh"),
        P("lev", "mesh"),
        P(None, "mesh"),
        P(None, "mesh"),
        P(None, "mesh"),
        P(None, "mesh"),
        P(None, "mesh"),
        P("mesh"),
        P("mesh", None),
        P("mesh"),
        P("mesh", None),
        P("mesh"),
    )
    out_specs = (P("lev", "mesh"), P("lev", "mesh"), P("lev", "mesh"))
    return jax.shard_map(body, mesh=mesh, in_specs=in_specs, out_specs=out_specs, check_vma=False)
```

```python
import functools

import jax
import jax.numpy as jnp
from jax import lax
from jax.experimental import pallas as pl
from jax.experimental.pallas import tpu as pltpu
from jax.sharding import PartitionSpec as P

MESH = pl.DeviceIdType.MESH
LANES = 128
SUB = 8
ALONG_LANES = lax.GatherDimensionNumbers(
    offset_dims=(),
    collapsed_slice_dims=(1,),
    start_index_map=(1,),
    operand_batching_dims=(0,),
    start_indices_batching_dims=(0,),
)


def pick(row, lanes):
    return lax.gather(
        row,
        lanes[..., None],
        ALONG_LANES,
        slice_sizes=(1, 1),
        mode=lax.GatherScatterMode.PROMISE_IN_BOUNDS,
    )


def tile(c):
    return pl.ds(pl.multiple_of(c * LANES, LANES), LANES)


def spread(row):
    return jnp.broadcast_to(row, (SUB, LANES))


def scan(first, last, load_rows, lookups, found, unroll):
    def one(lookup, held):
        row_of, lane_of = lookup

        def step(k, held):
            hit = row_of == k
            return tuple(jnp.where(hit, pick(r, lane_of), h) for r, h in zip(load_rows(k), held))

        return lax.fori_loop(first, last, step, tuple(held), unroll=unroll)

    return tuple(one(lookup, held) for lookup, held in zip(lookups, found))


def total_rows(x):
    return jnp.sum(x, axis=0, keepdims=True)


def kernel(
    n_mesh,
    n_lev,
    vel_h, thk_h, vor_h, wind_h, wts_h, eoe_h, eoc_h, coe_h, ew_h, invd_h, ehl_h, ehc_h, chl_h, chc_h,
    tend_h, tang_h, energy_h,
    vel, thk, vor, wind, wts, eoe, eoc, coe, ew, invd, ehl, ehc, chl, chc,
    tend, tang, energy, below, above, esend, erecv, csend, crecv, near, cell_near, cell_pick,
    load_sem, es_sem, er_sem, cs_sem, cr_sem, ls_sem, lr_sem, out_sem,
):
    levels, edges = vel.shape
    cells = energy.shape[1]
    blocks = ehl.shape[0]
    reach = blocks // 2
    halo_c = chl.shape[1]
    neoe, neoc = eoe.shape[0], eoc.shape[0]
    extra = neoe - SUB
    group = SUB // extra
    units = edges // (LANES * group)
    edge_rows = edges // LANES
    cell_rows = cells // LANES
    planes = 3 * levels
    me = lax.axis_index("mesh")
    lev = lax.axis_index("lev")

    def partner(o):
        offset = o + 1 if o < reach else reach - 1 - o
        return {"mesh": lax.rem(me + offset + n_mesh, n_mesh)}

    up = {"lev": lax.rem(lev + 1, n_lev)}
    down = {"lev": lax.rem(lev + n_lev - 1, n_lev)}

    barrier = pltpu.get_barrier_semaphore()
    for o in range(blocks):
        pl.semaphore_signal(barrier, inc=1, device_id=partner(o), device_id_type=MESH)
    pl.semaphore_signal(barrier, inc=1, device_id=up, device_id_type=MESH)
    pl.semaphore_signal(barrier, inc=1, device_id=down, device_id_type=MESH)

    pairs = [
        (ehl_h, ehl), (ehc_h, ehc), (vel_h, vel), (thk_h, thk), (vor_h, vor),
        (eoc_h, eoc), (eoe_h, eoe), (ew_h, ew), (wts_h, wts), (chl_h, chl), (chc_h, chc),
        (coe_h, coe), (invd_h, invd), (wind_h, wind),
    ]
    loads = []
    for i, (src, dst) in enumerate(pairs):
        copy = pltpu.make_async_copy(src, dst, load_sem.at[i])
        copy.start()
        loads.append(copy)
    esend[...] = jnp.zeros_like(esend)
    csend[...] = jnp.zeros_like(csend)
    cell_pick[...] = jnp.zeros_like(cell_pick)

    sublane = lax.broadcasted_iota(jnp.int32, (SUB, LANES), 0)
    lane = lax.broadcasted_iota(jnp.int32, (SUB, LANES), 1)
    blank = jnp.zeros((SUB, LANES), jnp.float32)

    def live(counts):
        most = jnp.zeros((SUB, LANES), jnp.int32)
        for o in range(blocks):
            most = jnp.where(sublane == o, counts[o], most)
        return lane < most

    def field_rows(k):
        return [
            spread(field[l : l + 1, tile(k)]) for field in (vel, thk, vor) for l in range(levels)
        ]

    def speed_rows(k):
        return [spread(vel[l : l + 1, tile(k)]) for l in range(levels)]

    def padded_rows(x):
        return jnp.concatenate([x, jnp.zeros((SUB - x.shape[0], LANES), x.dtype)], axis=0)

    for copy in loads[:5]:
        copy.wait()
    index = padded_rows(ehl[...])
    (packed,) = scan(
        0, edge_rows, field_rows, [(index >> 7, index & 127)], [(blank,) * planes], edge_rows
    )
    alive = live(ehc)
    for p in range(planes):
        block = jnp.where(alive, packed[p], 0.0)
        for o in range(blocks):
            esend[SUB * o + p : SUB * o + p + 1, :] = block[o : o + 1]

    pl.semaphore_wait(barrier, blocks + 2)
    edge_copies = []
    for o in range(blocks):
        rows = pl.ds(SUB * o, SUB)
        copy = pltpu.make_async_remote_copy(
            src_ref=esend.at[rows],
            dst_ref=erecv.at[rows],
            send_sem=es_sem.at[o],
            recv_sem=er_sem.at[o],
            device_id=partner(o),
            device_id_type=MESH,
        )
        copy.start()
        edge_copies.append(copy)
    rim_copies = []
    for i, (dst, target) in enumerate(((below, up), (above, down))):
        copy = pltpu.make_async_remote_copy(
            src_ref=vel,
            dst_ref=dst,
            send_sem=ls_sem.at[i],
            recv_sem=lr_sem.at[i],
            device_id=target,
            device_id_type=MESH,
        )
        copy.start()
        rim_copies.append(copy)

    loads[5].wait()
    cell_lookups = []
    for c in range(cell_rows):
        index = padded_rows(eoc[:, c * LANES : (c + 1) * LANES])
        cell_lookups.append((index >> 7, index & 127))
    found = scan(
        0, edge_rows, speed_rows, cell_lookups, [(blank,) * levels] * cell_rows, edge_rows
    )
    for c in range(cell_rows):
        for l in range(levels):
            cell_near[c * levels + l] = found[c][l]

    loads[6].wait()

    def unit_lookups(u):
        lookups = []
        for q in range(group):
            index = eoe[0:SUB, tile(u * group + q)]
            lookups.append((index >> 7, index & 127))
        index = jnp.concatenate(
            [eoe[SUB:neoe, tile(u * group + q)] for q in range(group)], axis=0
        )
        lookups.append((index >> 7, index & 127))
        return lookups

    def local_unit(u, carry):
        found = scan(
            0, edge_rows, field_rows, unit_lookups(u), [(blank,) * planes] * (group + 1), edge_rows
        )
        for g in range(group + 1):
            for p in range(planes):
                near[u, g * planes + p] = found[g][p]
        return carry

    lax.fori_loop(0, units, local_unit, 0)

    for copy in edge_copies:
        copy.wait()
    loads[7].wait()

    def halo_rows(count):
        def load(k):
            start = pl.multiple_of(SUB * (k - edge_rows), SUB)
            rows = erecv[pl.ds(start, SUB), :]
            return [spread(rows[p : p + 1]) for p in range(count)]

        return load

    found = [
        tuple(cell_near[c * levels + l] for l in range(levels)) for c in range(cell_rows)
    ]
    found = scan(edge_rows, edge_rows + blocks, halo_rows(levels), cell_lookups, found, blocks)
    for c in range(cell_rows):
        weight = padded_rows(ew[:, c * LANES : (c + 1) * LANES])
        energy[:, c * LANES : (c + 1) * LANES] = jnp.concatenate(
            [total_rows(weight * found[c][l] * found[c][l]) for l in range(levels)], axis=0
        )

    energy_out = pltpu.make_async_copy(energy, energy_h, out_sem.at[0])
    energy_out.start()

    for copy in loads[9:11]:
        copy.wait()
    cell_pick[0:blocks, 0:halo_c] = chl[...]
    index = cell_pick[...]

    def energy_rows(k):
        return [spread(energy[l : l + 1, tile(k)]) for l in range(levels)]

    (packed,) = scan(
        0, cell_rows, energy_rows, [(index >> 7, index & 127)], [(blank,) * levels], cell_rows
    )
    alive = live(chc)
    for l in range(levels):
        block = jnp.where(alive, packed[l], 0.0)
        for o in range(blocks):
            csend[SUB * o + l : SUB * o + l + 1, :] = block[o : o + 1]
    cell_copies = []
    for o in range(blocks):
        rows = pl.ds(SUB * o, SUB)
        copy = pltpu.make_async_remote_copy(
            src_ref=csend.at[rows],
            dst_ref=crecv.at[rows],
            send_sem=cs_sem.at[o],
            recv_sem=cr_sem.at[o],
            device_id=partner(o),
            device_id_type=MESH,
        )
        copy.start()
        cell_copies.append(copy)

    loads[8].wait()

    def halo_unit(u, carry):
        found = [
            tuple(near[u, g * planes + p] for p in range(planes)) for g in range(group + 1)
        ]
        found = scan(
            edge_rows, edge_rows + blocks, halo_rows(planes), unit_lookups(u), found, blocks
        )
        cols = [tile(u * group + q) for q in range(group)]
        few = jnp.concatenate([wts[SUB:neoe, c] for c in cols], axis=0)
        tangents = [[] for _ in cols]
        fluxes = [[] for _ in cols]
        for l in range(levels):
            own = [vor[l : l + 1, c] for c in cols]
            speed, height, potential = (found[group][f * levels + l] for f in range(3))
            own_few = jnp.concatenate(
                [jnp.broadcast_to(v, (extra, LANES)) for v in own], axis=0
            )
            moved_few = few * speed
            flux_few = moved_few * height * 0.5 * (own_few + potential)
            for q, c in enumerate(cols):
                speed, height, potential = (found[q][f * levels + l] for f in range(3))
                moved = wts[0:SUB, c] * speed
                flux = moved * height * 0.5 * (spread(own[q]) + potential)
                part = slice(extra * q, extra * (q + 1))
                tangents[q].append(total_rows(moved) + total_rows(moved_few[part]))
                fluxes[q].append(total_rows(flux) + total_rows(flux_few[part]))
        for q, c in enumerate(cols):
            tang[:, c] = jnp.concatenate(tangents[q], axis=0)
            tend[:, c] = jnp.concatenate(fluxes[q], axis=0)
        return carry

    lax.fori_loop(0, units, halo_unit, 0, unroll=2)
    tang_out = pltpu.make_async_copy(tang, tang_h, out_sem.at[1])
    tang_out.start()

    for copy in cell_copies + rim_copies + loads[11:]:
        copy.wait()
    ends = SUB // 2

    def end_unit(u, carry):
        cols = [tile(u * ends + q) for q in range(ends)]
        index = jnp.concatenate([coe[:, c] for c in cols], axis=0)
        far = index >= cells
        slot = index - cells
        place = (
            jnp.where(far, cell_rows + slot // halo_c, index >> 7),
            jnp.where(far, slot % halo_c, index & 127),
        )

        def received_rows(k):
            start = pl.multiple_of(SUB * (k - cell_rows), SUB)
            rows = crecv[pl.ds(start, SUB), :]
            return [spread(rows[l : l + 1]) for l in range(levels)]

        found = scan(0, cell_rows, energy_rows, [place], [(blank,) * levels], cell_rows)
        (found,) = scan(cell_rows, cell_rows + blocks, received_rows, [place], found, blocks)
        for q, c in enumerate(cols):
            rows = []
            for l in range(levels):
                gradient = (
                    found[l][2 * q + 1 : 2 * q + 2] - found[l][2 * q : 2 * q + 1]
                ) * invd[pl.ds(u * ends + q, 1), :]
                if l + 1 < levels:
                    over = vel[l + 1 : l + 2, c]
                else:
                    over = jnp.where(lev == n_lev - 1, 0.0, above[0:1, c])
                if l > 0:
                    under = vel[l - 1 : l, c]
                else:
                    under = jnp.where(lev == 0, 0.0, below[levels - 1 : levels, c])
                advect = -0.5 * wind[l : l + 1, c] * (over - under)
                rows.append((tend[l : l + 1, c] - gradient) + advect)
            tend[:, c] = jnp.concatenate(rows, axis=0)
        return carry

    lax.fori_loop(0, edge_rows // ends, end_unit, 0, unroll=edge_rows // ends)
    tend_out = pltpu.make_async_copy(tend, tend_h, out_sem.at[2])
    tend_out.start()
    for copy in (energy_out, tang_out, tend_out):
        copy.wait()


def place(*refs):
    *arrays, in_sem, out_sem = refs
    count = len(arrays) // 3
    sources, targets, held = (arrays[i * count : (i + 1) * count] for i in range(3))
    ins = [pltpu.make_async_copy(sources[i], held[i], in_sem.at[i]) for i in range(count)]
    outs = [pltpu.make_async_copy(held[i], targets[i], out_sem.at[i]) for i in range(count)]
    for copy in ins:
        copy.start()
    for arrived, leaving in zip(ins, outs):
        arrived.wait()
        leaving.start()
    for copy in outs:
        copy.wait()


def body(
    velocity,
    thickness,
    vorticity,
    vertical_wind,
    weights_on_edge,
    edges_on_edge,
    edges_on_cell,
    cells_on_edge,
    energy_weight,
    inverse_distance,
    edge_halo_list,
    edge_halo_count,
    cell_halo_list,
    cell_halo_count,
):
    levels, edges = velocity.shape
    cells = edges_on_cell.shape[1]
    blocks = edge_halo_list.shape[0]
    group = SUB // (edges_on_edge.shape[0] - SUB)
    units = edges // (LANES * group)
    args = [
        velocity, thickness, vorticity, vertical_wind, weights_on_edge, edges_on_edge,
        edges_on_cell, cells_on_edge, energy_weight, inverse_distance.reshape(-1, LANES),
        edge_halo_list, edge_halo_count, cell_halo_list, cell_halo_count,
    ]
    held = [
        pltpu.SMEM(a.shape, a.dtype) if a.ndim == 1 else pltpu.VMEM(a.shape, a.dtype) for a in args
    ]
    exchange = pltpu.VMEM((SUB * blocks, LANES), jnp.float32)
    dma = lambda n: pltpu.SemaphoreType.DMA((n,))
    results = (
        jax.ShapeDtypeStruct((levels, edges), jnp.float32),
        jax.ShapeDtypeStruct((levels, edges), jnp.float32),
        jax.ShapeDtypeStruct((levels, cells), jnp.float32),
    )
    anywhere = pl.BlockSpec(memory_space=pl.ANY)
    found = pl.pallas_call(
        functools.partial(kernel, lax.axis_size("mesh"), lax.axis_size("lev")),
        out_shape=results,
        in_specs=[anywhere] * len(args),
        out_specs=(anywhere,) * 3,
        scratch_shapes=held
        + [
            pltpu.VMEM((levels, edges), jnp.float32),
            pltpu.VMEM((levels, edges), jnp.float32),
            pltpu.VMEM((levels, cells), jnp.float32),
            pltpu.VMEM((levels, edges), jnp.float32),
            pltpu.VMEM((levels, edges), jnp.float32),
            exchange, exchange, exchange, exchange,
            pltpu.VMEM((units, (group + 1) * 3 * levels, SUB, LANES), jnp.float32),
            pltpu.VMEM((cells // LANES * levels, SUB, LANES), jnp.float32),
            pltpu.VMEM((SUB, LANES), jnp.int32),
            dma(len(args)), dma(blocks), dma(blocks), dma(blocks), dma(blocks), dma(2), dma(2), dma(3),
        ],
        compiler_params=pltpu.CompilerParams(collective_id=0, has_side_effects=True),
    )(*args)
    return pl.pallas_call(
        place,
        out_shape=results,
        in_specs=[anywhere] * 3,
        out_specs=(anywhere,) * 3,
        scratch_shapes=[pltpu.VMEM(r.shape, r.dtype) for r in results] + [dma(3), dma(3)],
    )(*found)


def solution(mesh):
    in_specs = (
        P("lev", "mesh"),
        P("lev", "mesh"),
        P("lev", "mesh"),
        P("lev", "mesh"),
        P(None, "mesh"),
        P(None, "mesh"),
        P(None, "mesh"),
        P(None, "mesh"),
        P(None, "mesh"),
        P("mesh"),
        P("mesh", None),
        P("mesh"),
        P("mesh", None),
        P("mesh"),
    )
    out_specs = (P("lev", "mesh"), P("lev", "mesh"), P("lev", "mesh"))
    return jax.shard_map(body, mesh=mesh, in_specs=in_specs, out_specs=out_specs, check_vma=False)
```

```python
import functools

import jax
import jax.numpy as jnp
from jax import lax
from jax.experimental import pallas as pl
from jax.experimental.pallas import tpu as pltpu
from jax.sharding import PartitionSpec as P

MESH = pl.DeviceIdType.MESH
LANES = 128
STEPS = 32767.0
HALF = 1 << 16
SUB = 8
ALONG_LANES = lax.GatherDimensionNumbers(
    offset_dims=(),
    collapsed_slice_dims=(1,),
    start_index_map=(1,),
    operand_batching_dims=(0,),
    start_indices_batching_dims=(0,),
)


def pick(row, lanes):
    return lax.gather(
        row,
        lanes[..., None],
        ALONG_LANES,
        slice_sizes=(1, 1),
        mode=lax.GatherScatterMode.PROMISE_IN_BOUNDS,
    )


def tile(c):
    return pl.ds(pl.multiple_of(c * LANES, LANES), LANES)


def spread(row):
    return jnp.broadcast_to(row, (SUB, LANES))


def scan(first, last, load_rows, lookups, found, unroll):
    def one(lookup, held):
        row_of, lane_of = lookup

        def step(k, held):
            hit = row_of == k
            return tuple(jnp.where(hit, pick(r, lane_of), h) for r, h in zip(load_rows(k), held))

        return lax.fori_loop(first, last, step, tuple(held), unroll=unroll)

    return tuple(one(lookup, held) for lookup, held in zip(lookups, found))


def coded(low, high):
    low, high = ((h * STEPS + 0.5).astype(jnp.int32) for h in (low, high))
    return low + high * HALF


def decoded(word):
    return (
        (word & (HALF - 1)).astype(jnp.float32),
        lax.shift_right_logical(word, 16).astype(jnp.float32),
    )


def total_rows(x):
    return jnp.sum(x, axis=0, keepdims=True)


def kernel(
    n_mesh,
    n_lev,
    vel_h, thk_h, vor_h, wind_h, wts_h, eoe_h, eoc_h, coe_h, ew_h, invd_h, ehl_h, ehc_h, chl_h, chc_h,
    tend_h, tang_h, energy_h,
    vel, thk, vor, wind, wts, eoe, eoc, coe, ew, invd, ehl, ehc, chl, chc,
    tend, tang, energy, below, above, esend, erecv, csend, crecv, near, near_code, code, code_halo, cell_near, cell_pick,
    load_sem, es_sem, er_sem, cs_sem, cr_sem, ls_sem, lr_sem, out_sem,
):
    levels, edges = vel.shape
    cells = energy.shape[1]
    blocks = ehl.shape[0]
    reach = blocks // 2
    halo_c = chl.shape[1]
    neoe, neoc = eoe.shape[0], eoc.shape[0]
    extra = neoe - SUB
    group = SUB // extra
    units = edges // (LANES * group)
    edge_rows = edges // LANES
    cell_rows = cells // LANES
    planes = 3 * levels
    exact = 2 * levels
    pairs_of = levels // 2
    me = lax.axis_index("mesh")
    lev = lax.axis_index("lev")

    def partner(o):
        offset = o + 1 if o < reach else reach - 1 - o
        return {"mesh": lax.rem(me + offset + n_mesh, n_mesh)}

    up = {"lev": lax.rem(lev + 1, n_lev)}
    down = {"lev": lax.rem(lev + n_lev - 1, n_lev)}

    barrier = pltpu.get_barrier_semaphore()
    for o in range(blocks):
        pl.semaphore_signal(barrier, inc=1, device_id=partner(o), device_id_type=MESH)
    pl.semaphore_signal(barrier, inc=1, device_id=up, device_id_type=MESH)
    pl.semaphore_signal(barrier, inc=1, device_id=down, device_id_type=MESH)

    pairs = [
        (ehl_h, ehl), (ehc_h, ehc), (vel_h, vel), (thk_h, thk), (vor_h, vor),
        (eoc_h, eoc), (eoe_h, eoe), (ew_h, ew), (wts_h, wts), (chl_h, chl), (chc_h, chc),
        (coe_h, coe), (invd_h, invd), (wind_h, wind),
    ]
    loads = []
    for i, (src, dst) in enumerate(pairs):
        copy = pltpu.make_async_copy(src, dst, load_sem.at[i])
        copy.start()
        loads.append(copy)
    esend[...] = jnp.zeros_like(esend)
    csend[...] = jnp.zeros_like(csend)
    cell_pick[...] = jnp.zeros_like(cell_pick)

    sublane = lax.broadcasted_iota(jnp.int32, (SUB, LANES), 0)
    lane = lax.broadcasted_iota(jnp.int32, (SUB, LANES), 1)
    blank = jnp.zeros((SUB, LANES), jnp.float32)

    def live(counts):
        most = jnp.zeros((SUB, LANES), jnp.int32)
        for o in range(blocks):
            most = jnp.where(sublane == o, counts[o], most)
        return lane < most

    def field_rows(k):
        return [
            spread(field[l : l + 1, tile(k)]) for field in (vel, thk, vor) for l in range(levels)
        ]

    def table_rows(k):
        rows = [spread(field[l : l + 1, tile(k)]) for field in (vel, vor) for l in range(levels)]
        return rows + [spread(code[i : i + 1, tile(k)]) for i in range(pairs_of)]

    def speed_rows(k):
        return [spread(vel[l : l + 1, tile(k)]) for l in range(levels)]

    def padded_rows(x):
        return jnp.concatenate([x, jnp.zeros((SUB - x.shape[0], LANES), x.dtype)], axis=0)

    for copy in loads[:5]:
        copy.wait()
    index = padded_rows(ehl[...])
    (packed,) = scan(
        0, edge_rows, field_rows, [(index >> 7, index & 127)], [(blank,) * planes], edge_rows
    )
    alive = live(ehc)
    for p in range(planes):
        block = jnp.where(alive, packed[p], 0.0)
        for o in range(blocks):
            esend[SUB * o + p : SUB * o + p + 1, :] = block[o : o + 1]

    pl.semaphore_wait(barrier, blocks + 2)
    edge_copies = []
    for o in range(blocks):
        rows = pl.ds(SUB * o, SUB)
        copy = pltpu.make_async_remote_copy(
            src_ref=esend.at[rows],
            dst_ref=erecv.at[rows],
            send_sem=es_sem.at[o],
            recv_sem=er_sem.at[o],
            device_id=partner(o),
            device_id_type=MESH,
        )
        copy.start()
        edge_copies.append(copy)
    rim_copies = []
    for i, (dst, target) in enumerate(((below, up), (above, down))):
        copy = pltpu.make_async_remote_copy(
            src_ref=vel,
            dst_ref=dst,
            send_sem=ls_sem.at[i],
            recv_sem=lr_sem.at[i],
            device_id=target,
            device_id_type=MESH,
        )
        copy.start()
        rim_copies.append(copy)

    for i in range(pairs_of):
        code[i : i + 1, :] = coded(thk[2 * i : 2 * i + 1, :], thk[2 * i + 1 : 2 * i + 2, :])

    loads[5].wait()
    cell_lookups = []
    for c in range(cell_rows):
        index = padded_rows(eoc[:, c * LANES : (c + 1) * LANES])
        cell_lookups.append((index >> 7, index & 127))
    found = scan(
        0, edge_rows, speed_rows, cell_lookups, [(blank,) * levels] * cell_rows, edge_rows
    )
    for c in range(cell_rows):
        for l in range(levels):
            cell_near[c * levels + l] = found[c][l]

    loads[6].wait()

    def unit_lookups(u):
        lookups = []
        for q in range(group):
            index = eoe[0:SUB, tile(u * group + q)]
            lookups.append((index >> 7, index & 127))
        index = jnp.concatenate(
            [eoe[SUB:neoe, tile(u * group + q)] for q in range(group)], axis=0
        )
        lookups.append((index >> 7, index & 127))
        return lookups

    none = (blank,) * exact + (jnp.zeros((SUB, LANES), jnp.int32),) * pairs_of

    def local_unit(u, carry):
        found = scan(
            0, edge_rows, table_rows, unit_lookups(u), [none] * (group + 1), edge_rows
        )
        for g in range(group + 1):
            for p in range(exact):
                near[u, g * exact + p] = found[g][p]
            for i in range(pairs_of):
                near_code[u, g * pairs_of + i] = found[g][exact + i]
        return carry

    lax.fori_loop(0, units, local_unit, 0, unroll=2)

    for copy in edge_copies:
        copy.wait()
    loads[7].wait()

    for o in range(blocks):
        for i in range(pairs_of):
            first = SUB * o + levels + 2 * i
            code_halo[SUB * o + i : SUB * o + i + 1, :] = coded(
                erecv[first : first + 1, :], erecv[first + 1 : first + 2, :]
            )

    def halo_rows(which, codes):
        def load(k):
            start = pl.multiple_of(SUB * (k - edge_rows), SUB)
            rows = erecv[pl.ds(start, SUB), :]
            taken = [spread(rows[p : p + 1]) for p in which]
            if codes:
                rows = code_halo[pl.ds(start, SUB), :]
                taken += [spread(rows[i : i + 1]) for i in range(pairs_of)]
            return taken

        return load

    found = [
        tuple(cell_near[c * levels + l] for l in range(levels)) for c in range(cell_rows)
    ]
    found = scan(edge_rows, edge_rows + blocks, halo_rows(range(levels), False), cell_lookups, found, blocks)
    for c in range(cell_rows):
        weight = padded_rows(ew[:, c * LANES : (c + 1) * LANES])
        energy[:, c * LANES : (c + 1) * LANES] = jnp.concatenate(
            [total_rows(weight * found[c][l] * found[c][l]) for l in range(levels)], axis=0
        )

    energy_out = pltpu.make_async_copy(energy, energy_h, out_sem.at[0])
    energy_out.start()

    for copy in loads[9:11]:
        copy.wait()
    cell_pick[0:blocks, 0:halo_c] = chl[...]
    index = cell_pick[...]

    def energy_rows(k):
        return [spread(energy[l : l + 1, tile(k)]) for l in range(levels)]

    (packed,) = scan(
        0, cell_rows, energy_rows, [(index >> 7, index & 127)], [(blank,) * levels], cell_rows
    )
    alive = live(chc)
    for l in range(levels):
        block = jnp.where(alive, packed[l], 0.0)
        for o in range(blocks):
            csend[SUB * o + l : SUB * o + l + 1, :] = block[o : o + 1]
    cell_copies = []
    for o in range(blocks):
        rows = pl.ds(SUB * o, SUB)
        copy = pltpu.make_async_remote_copy(
            src_ref=csend.at[rows],
            dst_ref=crecv.at[rows],
            send_sem=cs_sem.at[o],
            recv_sem=cr_sem.at[o],
            device_id=partner(o),
            device_id_type=MESH,
        )
        copy.start()
        cell_copies.append(copy)

    loads[8].wait()

    table_halo = halo_rows(list(range(levels)) + list(range(2 * levels, planes)), True)

    def halo_unit(u, carry):
        found = [
            tuple(near[u, g * exact + p] for p in range(exact))
            + tuple(near_code[u, g * pairs_of + i] for i in range(pairs_of))
            for g in range(group + 1)
        ]
        found = scan(
            edge_rows, edge_rows + blocks, table_halo, unit_lookups(u), found, blocks
        )
        heights = [sum((decoded(f[exact + i]) for i in range(pairs_of)), ()) for f in found]
        cols = [tile(u * group + q) for q in range(group)]
        few = jnp.concatenate([wts[SUB:neoe, c] for c in cols], axis=0)
        tangents = [[] for _ in cols]
        fluxes = [[] for _ in cols]
        for l in range(levels):
            own = [vor[l : l + 1, c] for c in cols]
            speed, potential = found[group][l], found[group][levels + l]
            own_few = jnp.concatenate(
                [jnp.broadcast_to(v, (extra, LANES)) for v in own], axis=0
            )
            moved_few = few * speed
            flux_few = moved_few * heights[group][l] * (0.5 / STEPS) * (own_few + potential)
            for q, c in enumerate(cols):
                speed, potential = found[q][l], found[q][levels + l]
                moved = wts[0:SUB, c] * speed
                flux = moved * heights[q][l] * (0.5 / STEPS) * (spread(own[q]) + potential)
                part = slice(extra * q, extra * (q + 1))
                tangents[q].append(total_rows(moved) + total_rows(moved_few[part]))
                fluxes[q].append(total_rows(flux) + total_rows(flux_few[part]))
        for q, c in enumerate(cols):
            tang[:, c] = jnp.concatenate(tangents[q], axis=0)
            tend[:, c] = jnp.concatenate(fluxes[q], axis=0)
        return carry

    lax.fori_loop(0, units, halo_unit, 0, unroll=units)
    tang_out = pltpu.make_async_copy(tang, tang_h, out_sem.at[1])
    tang_out.start()

    for copy in cell_copies + rim_copies + loads[11:]:
        copy.wait()
    ends = SUB // 2

    def end_unit(u, carry):
        cols = [tile(u * ends + q) for q in range(ends)]
        index = jnp.concatenate([coe[:, c] for c in cols], axis=0)
        far = index >= cells
        slot = index - cells
        place = (
            jnp.where(far, cell_rows + slot // halo_c, index >> 7),
            jnp.where(far, slot % halo_c, index & 127),
        )

        def received_rows(k):
            start = pl.multiple_of(SUB * (k - cell_rows), SUB)
            rows = crecv[pl.ds(start, SUB), :]
            return [spread(rows[l : l + 1]) for l in range(levels)]

        found = scan(0, cell_rows, energy_rows, [place], [(blank,) * levels], cell_rows)
        (found,) = scan(cell_rows, cell_rows + blocks, received_rows, [place], found, blocks)
        for q, c in enumerate(cols):
            rows = []
            for l in range(levels):
                gradient = (
                    found[l][2 * q + 1 : 2 * q + 2] - found[l][2 * q : 2 * q + 1]
                ) * invd[pl.ds(u * ends + q, 1), :]
                if l + 1 < levels:
                    over = vel[l + 1 : l + 2, c]
                else:
                    over = jnp.where(lev == n_lev - 1, 0.0, above[0:1, c])
                if l > 0:
                    under = vel[l - 1 : l, c]
                else:
                    under = jnp.where(lev == 0, 0.0, below[levels - 1 : levels, c])
                advect = -0.5 * wind[l : l + 1, c] * (over - under)
                rows.append((tend[l : l + 1, c] - gradient) + advect)
            tend[:, c] = jnp.concatenate(rows, axis=0)
        return carry

    lax.fori_loop(0, edge_rows // ends, end_unit, 0, unroll=edge_rows // ends)
    tend_out = pltpu.make_async_copy(tend, tend_h, out_sem.at[2])
    tend_out.start()
    for copy in (energy_out, tang_out, tend_out):
        copy.wait()


def place(*refs):
    *arrays, in_sem, out_sem = refs
    count = len(arrays) // 3
    sources, targets, held = (arrays[i * count : (i + 1) * count] for i in range(3))
    ins = [pltpu.make_async_copy(sources[i], held[i], in_sem.at[i]) for i in range(count)]
    outs = [pltpu.make_async_copy(held[i], targets[i], out_sem.at[i]) for i in range(count)]
    for copy in ins:
        copy.start()
    for arrived, leaving in zip(ins, outs):
        arrived.wait()
        leaving.start()
    for copy in outs:
        copy.wait()


def body(
    velocity,
    thickness,
    vorticity,
    vertical_wind,
    weights_on_edge,
    edges_on_edge,
    edges_on_cell,
    cells_on_edge,
    energy_weight,
    inverse_distance,
    edge_halo_list,
    edge_halo_count,
    cell_halo_list,
    cell_halo_count,
):
    levels, edges = velocity.shape
    cells = edges_on_cell.shape[1]
    blocks = edge_halo_list.shape[0]
    group = SUB // (edges_on_edge.shape[0] - SUB)
    units = edges // (LANES * group)
    args = [
        velocity, thickness, vorticity, vertical_wind, weights_on_edge, edges_on_edge,
        edges_on_cell, cells_on_edge, energy_weight, inverse_distance.reshape(-1, LANES),
        edge_halo_list, edge_halo_count, cell_halo_list, cell_halo_count,
    ]
    held = [
        pltpu.SMEM(a.shape, a.dtype) if a.ndim == 1 else pltpu.VMEM(a.shape, a.dtype) for a in args
    ]
    exchange = pltpu.VMEM((SUB * blocks, LANES), jnp.float32)
    dma = lambda n: pltpu.SemaphoreType.DMA((n,))
    results = (
        jax.ShapeDtypeStruct((levels, edges), jnp.float32),
        jax.ShapeDtypeStruct((levels, edges), jnp.float32),
        jax.ShapeDtypeStruct((levels, cells), jnp.float32),
    )
    anywhere = pl.BlockSpec(memory_space=pl.ANY)
    found = pl.pallas_call(
        functools.partial(kernel, lax.axis_size("mesh"), lax.axis_size("lev")),
        out_shape=results,
        in_specs=[anywhere] * len(args),
        out_specs=(anywhere,) * 3,
        scratch_shapes=held
        + [
            pltpu.VMEM((levels, edges), jnp.float32),
            pltpu.VMEM((levels, edges), jnp.float32),
            pltpu.VMEM((levels, cells), jnp.float32),
            pltpu.VMEM((levels, edges), jnp.float32),
            pltpu.VMEM((levels, edges), jnp.float32),
            exchange, exchange, exchange, exchange,
            pltpu.VMEM((units, (group + 1) * 2 * levels, SUB, LANES), jnp.float32),
            pltpu.VMEM((units, (group + 1) * (levels // 2), SUB, LANES), jnp.int32),
            pltpu.VMEM((levels // 2, edges), jnp.int32),
            pltpu.VMEM((SUB * blocks, LANES), jnp.int32),
            pltpu.VMEM((cells // LANES * levels, SUB, LANES), jnp.float32),
            pltpu.VMEM((SUB, LANES), jnp.int32),
            dma(len(args)), dma(blocks), dma(blocks), dma(blocks), dma(blocks), dma(2), dma(2), dma(3),
        ],
        compiler_params=pltpu.CompilerParams(collective_id=0, has_side_effects=True),
    )(*args)
    return pl.pallas_call(
        place,
        out_shape=results,
        in_specs=[anywhere] * 3,
        out_specs=(anywhere,) * 3,
        scratch_shapes=[pltpu.VMEM(r.shape, r.dtype) for r in results] + [dma(3), dma(3)],
    )(*found)


def solution(mesh):
    in_specs = (
        P("lev", "mesh"),
        P("lev", "mesh"),
        P("lev", "mesh"),
        P("lev", "mesh"),
        P(None, "mesh"),
        P(None, "mesh"),
        P(None, "mesh"),
        P(None, "mesh"),
        P(None, "mesh"),
        P("mesh"),
        P("mesh", None),
        P("mesh"),
        P("mesh", None),
        P("mesh"),
    )
    out_specs = (P("lev", "mesh"), P("lev", "mesh"), P("lev", "mesh"))
    return jax.shard_map(body, mesh=mesh, in_specs=in_specs, out_specs=out_specs, check_vma=False)
```

```python
import functools

import jax
import jax.numpy as jnp
from jax import lax
from jax.experimental import pallas as pl
from jax.experimental.pallas import tpu as pltpu
from jax.sharding import PartitionSpec as P

MESH = pl.DeviceIdType.MESH
LANES = 128
STEPS = 32767.0
HALF = 1 << 16
SUB = 8
ALONG_LANES = lax.GatherDimensionNumbers(
    offset_dims=(),
    collapsed_slice_dims=(1,),
    start_index_map=(1,),
    operand_batching_dims=(0,),
    start_indices_batching_dims=(0,),
)


def pick(row, lanes):
    return lax.gather(
        row,
        lanes[..., None],
        ALONG_LANES,
        slice_sizes=(1, 1),
        mode=lax.GatherScatterMode.PROMISE_IN_BOUNDS,
    )


def tile(c):
    return pl.ds(pl.multiple_of(c * LANES, LANES), LANES)


def spread(row):
    return jnp.broadcast_to(row, (SUB, LANES))


def scan(first, last, load_rows, lookups, found, unroll):
    def one(lookup, held):
        row_of, lane_of = lookup

        def step(k, held):
            hit = row_of == k
            return tuple(jnp.where(hit, pick(r, lane_of), h) for r, h in zip(load_rows(k), held))

        return lax.fori_loop(first, last, step, tuple(held), unroll=unroll)

    return tuple(one(lookup, held) for lookup, held in zip(lookups, found))


def coded(low, high):
    low, high = ((h * STEPS + 0.5).astype(jnp.int32) for h in (low, high))
    return low + high * HALF


def decoded(word):
    return (
        (word & (HALF - 1)).astype(jnp.float32),
        lax.shift_right_logical(word, 16).astype(jnp.float32),
    )


def total_rows(x):
    return jnp.sum(x, axis=0, keepdims=True)


def kernel(
    n_mesh,
    n_lev,
    vel_h, thk_h, vor_h, wind_h, wts_h, eoe_h, eoc_h, coe_h, ew_h, invd_h, ehl_h, ehc_h, chl_h, chc_h,
    tend_h, tang_h, energy_h,
    vel, thk, vor, wind, wts, eoe, eoc, coe, ew, invd, ehl, ehc, chl, chc,
    tend, tang, energy, below, above, esend, erecv, csend, crecv, near, near_code, code, code_halo, cell_near, cell_pick,
    load_sem, es_sem, er_sem, cs_sem, cr_sem, ls_sem, lr_sem, out_sem,
):
    levels, edges = vel.shape
    cells = energy.shape[1]
    blocks = ehl.shape[0]
    reach = blocks // 2
    halo_c = chl.shape[1]
    neoe, neoc = eoe.shape[0], eoc.shape[0]
    extra = neoe - SUB
    group = SUB // extra
    units = edges // (LANES * group)
    edge_rows = edges // LANES
    cell_rows = cells // LANES
    planes = 3 * levels
    exact = 2 * levels
    pairs_of = levels // 2
    me = lax.axis_index("mesh")
    lev = lax.axis_index("lev")

    def partner(o):
        offset = o + 1 if o < reach else reach - 1 - o
        return {"mesh": lax.rem(me + offset + n_mesh, n_mesh)}

    up = {"lev": lax.rem(lev + 1, n_lev)}
    down = {"lev": lax.rem(lev + n_lev - 1, n_lev)}

    barrier = pltpu.get_barrier_semaphore()
    for o in range(blocks):
        pl.semaphore_signal(barrier, inc=1, device_id=partner(o), device_id_type=MESH)
    pl.semaphore_signal(barrier, inc=1, device_id=up, device_id_type=MESH)
    pl.semaphore_signal(barrier, inc=1, device_id=down, device_id_type=MESH)

    pairs = [
        (ehl_h, ehl), (ehc_h, ehc), (vel_h, vel), (thk_h, thk), (vor_h, vor),
        (eoc_h, eoc), (eoe_h, eoe), (ew_h, ew), (wts_h, wts), (chl_h, chl), (chc_h, chc),
        (coe_h, coe), (invd_h, invd), (wind_h, wind),
    ]
    loads = []
    for i, (src, dst) in enumerate(pairs):
        copy = pltpu.make_async_copy(src, dst, load_sem.at[i])
        copy.start()
        loads.append(copy)
    esend[...] = jnp.zeros_like(esend)
    csend[...] = jnp.zeros_like(csend)
    cell_pick[...] = jnp.zeros_like(cell_pick)

    sublane = lax.broadcasted_iota(jnp.int32, (SUB, LANES), 0)
    lane = lax.broadcasted_iota(jnp.int32, (SUB, LANES), 1)
    blank = jnp.zeros((SUB, LANES), jnp.float32)

    def live(counts):
        most = jnp.zeros((SUB, LANES), jnp.int32)
        for o in range(blocks):
            most = jnp.where(sublane == o, counts[o], most)
        return lane < most

    def field_rows(k):
        return [
            spread(field[l : l + 1, tile(k)]) for field in (vel, thk, vor) for l in range(levels)
        ]

    def table_rows(k):
        rows = [spread(field[l : l + 1, tile(k)]) for field in (vel, vor) for l in range(levels)]
        return rows + [spread(code[i : i + 1, tile(k)]) for i in range(pairs_of)]

    def speed_rows(k):
        return [spread(vel[l : l + 1, tile(k)]) for l in range(levels)]

    def padded_rows(x):
        return jnp.concatenate([x, jnp.zeros((SUB - x.shape[0], LANES), x.dtype)], axis=0)

    for copy in loads[:5]:
        copy.wait()
    index = padded_rows(ehl[...])
    (packed,) = scan(
        0, edge_rows, field_rows, [(index >> 7, index & 127)], [(blank,) * planes], edge_rows
    )
    alive = live(ehc)
    for p in range(planes):
        block = jnp.where(alive, packed[p], 0.0)
        for o in range(blocks):
            esend[SUB * o + p : SUB * o + p + 1, :] = block[o : o + 1]

    for i in range(pairs_of):
        code[i : i + 1, :] = coded(thk[2 * i : 2 * i + 1, :], thk[2 * i + 1 : 2 * i + 2, :])

    loads[6].wait()

    def unit_lookups(u):
        lookups = []
        for q in range(group):
            index = eoe[0:SUB, tile(u * group + q)]
            lookups.append((index >> 7, index & 127))
        index = jnp.concatenate(
            [eoe[SUB:neoe, tile(u * group + q)] for q in range(group)], axis=0
        )
        lookups.append((index >> 7, index & 127))
        return lookups

    none = (blank,) * exact + (jnp.zeros((SUB, LANES), jnp.int32),) * pairs_of

    def local_unit(u, carry):
        found = scan(
            0, edge_rows, table_rows, unit_lookups(u), [none] * (group + 1), edge_rows
        )
        for g in range(group + 1):
            for p in range(exact):
                near[u, g * exact + p] = found[g][p]
            for i in range(pairs_of):
                near_code[u, g * pairs_of + i] = found[g][exact + i]
        return carry

    early, middle = units // 3, 2 * units // 3
    lax.fori_loop(0, early, local_unit, 0, unroll=2)

    pl.semaphore_wait(barrier, blocks + 2)
    edge_copies = []
    for o in range(blocks):
        rows = pl.ds(SUB * o, SUB)
        copy = pltpu.make_async_remote_copy(
            src_ref=esend.at[rows],
            dst_ref=erecv.at[rows],
            send_sem=es_sem.at[o],
            recv_sem=er_sem.at[o],
            device_id=partner(o),
            device_id_type=MESH,
        )
        copy.start()
        edge_copies.append(copy)
    rim_copies = []
    for i, (dst, target) in enumerate(((below, up), (above, down))):
        copy = pltpu.make_async_remote_copy(
            src_ref=vel,
            dst_ref=dst,
            send_sem=ls_sem.at[i],
            recv_sem=lr_sem.at[i],
            device_id=target,
            device_id_type=MESH,
        )
        copy.start()
        rim_copies.append(copy)

    loads[5].wait()
    cell_lookups = []
    for c in range(cell_rows):
        index = padded_rows(eoc[:, c * LANES : (c + 1) * LANES])
        cell_lookups.append((index >> 7, index & 127))
    found = scan(
        0, edge_rows, speed_rows, cell_lookups, [(blank,) * levels] * cell_rows, edge_rows
    )
    for c in range(cell_rows):
        for l in range(levels):
            cell_near[c * levels + l] = found[c][l]

    lax.fori_loop(early, middle, local_unit, 0, unroll=2)

    for copy in edge_copies:
        copy.wait()
    loads[7].wait()

    for o in range(blocks):
        for i in range(pairs_of):
            first = SUB * o + levels + 2 * i
            code_halo[SUB * o + i : SUB * o + i + 1, :] = coded(
                erecv[first : first + 1, :], erecv[first + 1 : first + 2, :]
            )

    def halo_rows(which, codes):
        def load(k):
            start = pl.multiple_of(SUB * (k - edge_rows), SUB)
            rows = erecv[pl.ds(start, SUB), :]
            taken = [spread(rows[p : p + 1]) for p in which]
            if codes:
                rows = code_halo[pl.ds(start, SUB), :]
                taken += [spread(rows[i : i + 1]) for i in range(pairs_of)]
            return taken

        return load

    found = [
        tuple(cell_near[c * levels + l] for l in range(levels)) for c in range(cell_rows)
    ]
    found = scan(edge_rows, edge_rows + blocks, halo_rows(range(levels), False), cell_lookups, found, blocks)
    for c in range(cell_rows):
        weight = padded_rows(ew[:, c * LANES : (c + 1) * LANES])
        energy[:, c * LANES : (c + 1) * LANES] = jnp.concatenate(
            [total_rows(weight * found[c][l] * found[c][l]) for l in range(levels)], axis=0
        )

    energy_out = pltpu.make_async_copy(energy, energy_h, out_sem.at[0])
    energy_out.start()

    for copy in loads[9:11]:
        copy.wait()
    cell_pick[0:blocks, 0:halo_c] = chl[...]
    index = cell_pick[...]

    def energy_rows(k):
        return [spread(energy[l : l + 1, tile(k)]) for l in range(levels)]

    (packed,) = scan(
        0, cell_rows, energy_rows, [(index >> 7, index & 127)], [(blank,) * levels], cell_rows
    )
    alive = live(chc)
    for l in range(levels):
        block = jnp.where(alive, packed[l], 0.0)
        for o in range(blocks):
            csend[SUB * o + l : SUB * o + l + 1, :] = block[o : o + 1]
    cell_copies = []
    for o in range(blocks):
        rows = pl.ds(SUB * o, SUB)
        copy = pltpu.make_async_remote_copy(
            src_ref=csend.at[rows],
            dst_ref=crecv.at[rows],
            send_sem=cs_sem.at[o],
            recv_sem=cr_sem.at[o],
            device_id=partner(o),
            device_id_type=MESH,
        )
        copy.start()
        cell_copies.append(copy)

    lax.fori_loop(middle, units, local_unit, 0, unroll=2)

    loads[8].wait()

    table_halo = halo_rows(list(range(levels)) + list(range(2 * levels, planes)), True)

    def halo_unit(u, carry):
        found = [
            tuple(near[u, g * exact + p] for p in range(exact))
            + tuple(near_code[u, g * pairs_of + i] for i in range(pairs_of))
            for g in range(group + 1)
        ]
        found = scan(
            edge_rows, edge_rows + blocks, table_halo, unit_lookups(u), found, blocks
        )
        heights = [sum((decoded(f[exact + i]) for i in range(pairs_of)), ()) for f in found]
        cols = [tile(u * group + q) for q in range(group)]
        few = jnp.concatenate([wts[SUB:neoe, c] for c in cols], axis=0)
        tangents = [[] for _ in cols]
        fluxes = [[] for _ in cols]
        for l in range(levels):
            own = [vor[l : l + 1, c] for c in cols]
            speed, potential = found[group][l], found[group][levels + l]
            own_few = jnp.concatenate(
                [jnp.broadcast_to(v, (extra, LANES)) for v in own], axis=0
            )
            moved_few = few * speed
            flux_few = moved_few * heights[group][l] * (0.5 / STEPS) * (own_few + potential)
            for q, c in enumerate(cols):
                speed, potential = found[q][l], found[q][levels + l]
                moved = wts[0:SUB, c] * speed
                flux = moved * heights[q][l] * (0.5 / STEPS) * (spread(own[q]) + potential)
                part = slice(extra * q, extra * (q + 1))
                tangents[q].append(total_rows(moved) + total_rows(moved_few[part]))
                fluxes[q].append(total_rows(flux) + total_rows(flux_few[part]))
        for q, c in enumerate(cols):
            tang[:, c] = jnp.concatenate(tangents[q], axis=0)
            tend[:, c] = jnp.concatenate(fluxes[q], axis=0)
        return carry

    lax.fori_loop(0, units, halo_unit, 0, unroll=units)
    tang_out = pltpu.make_async_copy(tang, tang_h, out_sem.at[1])
    tang_out.start()

    for copy in rim_copies + loads[11:]:
        copy.wait()
    ends = SUB // 2
    end_units = edge_rows // ends
    places = []
    for u in range(end_units):
        index = jnp.concatenate([coe[:, tile(u * ends + q)] for q in range(ends)], axis=0)
        far = index >= cells
        slot = index - cells
        places.append((
            jnp.where(far, cell_rows + slot // halo_c, index >> 7),
            jnp.where(far, slot % halo_c, index & 127),
        ))
    found = scan(
        0, cell_rows, energy_rows, places, [(blank,) * levels] * end_units, cell_rows
    )
    for c in range(edge_rows):
        col = tile(c)
        for l in range(levels):
            if l + 1 < levels:
                over = vel[l + 1 : l + 2, col]
            else:
                over = jnp.where(lev == n_lev - 1, 0.0, above[0:1, col])
            if l > 0:
                under = vel[l - 1 : l, col]
            else:
                under = jnp.where(lev == 0, 0.0, below[levels - 1 : levels, col])
            wind[l : l + 1, col] = -0.5 * wind[l : l + 1, col] * (over - under)

    def received_rows(k):
        start = pl.multiple_of(SUB * (k - cell_rows), SUB)
        rows = crecv[pl.ds(start, SUB), :]
        return [spread(rows[l : l + 1]) for l in range(levels)]

    for copy in cell_copies:
        copy.wait()
    found = scan(cell_rows, cell_rows + blocks, received_rows, places, found, blocks)
    for c in range(edge_rows):
        u, q = c // ends, c % ends
        gradient = jnp.concatenate(
            [
                found[u][l][2 * q + 1 : 2 * q + 2] - found[u][l][2 * q : 2 * q + 1]
                for l in range(levels)
            ],
            axis=0,
        ) * invd[c : c + 1, :]
        tend[:, tile(c)] = (tend[:, tile(c)] - gradient) + wind[:, tile(c)]

    tend_out = pltpu.make_async_copy(tend, tend_h, out_sem.at[2])
    tend_out.start()
    for copy in (energy_out, tang_out, tend_out):
        copy.wait()


def place(*refs):
    *arrays, in_sem, out_sem = refs
    count = len(arrays) // 3
    sources, targets, held = (arrays[i * count : (i + 1) * count] for i in range(3))
    ins = [pltpu.make_async_copy(sources[i], held[i], in_sem.at[i]) for i in range(count)]
    outs = [pltpu.make_async_copy(held[i], targets[i], out_sem.at[i]) for i in range(count)]
    for copy in ins:
        copy.start()
    for arrived, leaving in zip(ins, outs):
        arrived.wait()
        leaving.start()
    for copy in outs:
        copy.wait()


def body(
    velocity,
    thickness,
    vorticity,
    vertical_wind,
    weights_on_edge,
    edges_on_edge,
    edges_on_cell,
    cells_on_edge,
    energy_weight,
    inverse_distance,
    edge_halo_list,
    edge_halo_count,
    cell_halo_list,
    cell_halo_count,
):
    levels, edges = velocity.shape
    cells = edges_on_cell.shape[1]
    blocks = edge_halo_list.shape[0]
    group = SUB // (edges_on_edge.shape[0] - SUB)
    units = edges // (LANES * group)
    args = [
        velocity, thickness, vorticity, vertical_wind, weights_on_edge, edges_on_edge,
        edges_on_cell, cells_on_edge, energy_weight, inverse_distance.reshape(-1, LANES),
        edge_halo_list, edge_halo_count, cell_halo_list, cell_halo_count,
    ]
    held = [
        pltpu.SMEM(a.shape, a.dtype) if a.ndim == 1 else pltpu.VMEM(a.shape, a.dtype) for a in args
    ]
    exchange = pltpu.VMEM((SUB * blocks, LANES), jnp.float32)
    dma = lambda n: pltpu.SemaphoreType.DMA((n,))
    results = (
        jax.ShapeDtypeStruct((levels, edges), jnp.float32),
        jax.ShapeDtypeStruct((levels, edges), jnp.float32),
        jax.ShapeDtypeStruct((levels, cells), jnp.float32),
    )
    anywhere = pl.BlockSpec(memory_space=pl.ANY)
    found = pl.pallas_call(
        functools.partial(kernel, lax.axis_size("mesh"), lax.axis_size("lev")),
        out_shape=results,
        in_specs=[anywhere] * len(args),
        out_specs=(anywhere,) * 3,
        scratch_shapes=held
        + [
            pltpu.VMEM((levels, edges), jnp.float32),
            pltpu.VMEM((levels, edges), jnp.float32),
            pltpu.VMEM((levels, cells), jnp.float32),
            pltpu.VMEM((levels, edges), jnp.float32),
            pltpu.VMEM((levels, edges), jnp.float32),
            exchange, exchange, exchange, exchange,
            pltpu.VMEM((units, (group + 1) * 2 * levels, SUB, LANES), jnp.float32),
            pltpu.VMEM((units, (group + 1) * (levels // 2), SUB, LANES), jnp.int32),
            pltpu.VMEM((levels // 2, edges), jnp.int32),
            pltpu.VMEM((SUB * blocks, LANES), jnp.int32),
            pltpu.VMEM((cells // LANES * levels, SUB, LANES), jnp.float32),
            pltpu.VMEM((SUB, LANES), jnp.int32),
            dma(len(args)), dma(blocks), dma(blocks), dma(blocks), dma(blocks), dma(2), dma(2), dma(3),
        ],
        compiler_params=pltpu.CompilerParams(collective_id=0, has_side_effects=True),
    )(*args)
    return pl.pallas_call(
        place,
        out_shape=results,
        in_specs=[anywhere] * 3,
        out_specs=(anywhere,) * 3,
        scratch_shapes=[pltpu.VMEM(r.shape, r.dtype) for r in results] + [dma(3), dma(3)],
    )(*found)


def solution(mesh):
    in_specs = (
        P("lev", "mesh"),
        P("lev", "mesh"),
        P("lev", "mesh"),
        P("lev", "mesh"),
        P(None, "mesh"),
        P(None, "mesh"),
        P(None, "mesh"),
        P(None, "mesh"),
        P(None, "mesh"),
        P("mesh"),
        P("mesh", None),
        P("mesh"),
        P("mesh", None),
        P("mesh"),
    )
    out_specs = (P("lev", "mesh"), P("lev", "mesh"), P("lev", "mesh"))
    return jax.shard_map(body, mesh=mesh, in_specs=in_specs, out_specs=out_specs, check_vma=False)
```

```python
import functools

import jax
import jax.numpy as jnp
from jax import lax
from jax.experimental import pallas as pl
from jax.experimental.pallas import tpu as pltpu
from jax.sharding import PartitionSpec as P

MESH = pl.DeviceIdType.MESH
LANES = 128
STEPS = 32767.0
HALF = 1 << 16
SUB = 8
ALONG_LANES = lax.GatherDimensionNumbers(
    offset_dims=(),
    collapsed_slice_dims=(1,),
    start_index_map=(1,),
    operand_batching_dims=(0,),
    start_indices_batching_dims=(0,),
)


def pick(row, lanes):
    return lax.gather(
        row,
        lanes[..., None],
        ALONG_LANES,
        slice_sizes=(1, 1),
        mode=lax.GatherScatterMode.PROMISE_IN_BOUNDS,
    )


def tile(c):
    return pl.ds(pl.multiple_of(c * LANES, LANES), LANES)


def spread(row):
    return jnp.broadcast_to(row, (SUB, LANES))


def scan(first, last, load_rows, lookups, found, unroll):
    def one(lookup, held):
        row_of, lane_of = lookup

        def step(k, held):
            hit = row_of == k
            return tuple(jnp.where(hit, pick(r, lane_of), h) for r, h in zip(load_rows(k), held))

        return lax.fori_loop(first, last, step, tuple(held), unroll=unroll)

    return tuple(one(lookup, held) for lookup, held in zip(lookups, found))


def coded(low, high):
    low, high = ((h * STEPS + 0.5).astype(jnp.int32) for h in (low, high))
    return low + high * HALF


def decoded(word):
    return (
        (word & (HALF - 1)).astype(jnp.float32),
        lax.shift_right_logical(word, 16).astype(jnp.float32),
    )


def total_rows(x):
    return jnp.sum(x, axis=0, keepdims=True)


def kernel(
    n_mesh,
    n_lev,
    vel_h, thk_h, vor_h, wind_h, wts_h, eoe_h, eoc_h, coe_h, ew_h, invd_h, ehl_h, ehc_h, chl_h, chc_h,
    tend_h, tang_h, energy_h,
    vel, thk, vor, wind, wts, eoe, eoc, coe, ew, invd, ehl, ehc, chl, chc,
    tend, tang, energy, below, above, esend, erecv, csend, crecv, near, near_code, code, code_halo, cell_pick,
    load_sem, es_sem, er_sem, cs_sem, cr_sem, ls_sem, lr_sem, out_sem,
):
    levels, edges = vel.shape
    cells = energy.shape[1]
    blocks = ehl.shape[0]
    reach = blocks // 2
    halo_c = chl.shape[1]
    neoe, neoc = eoe.shape[0], eoc.shape[0]
    extra = neoe - SUB
    group = SUB // extra
    units = edges // (LANES * group)
    edge_rows = edges // LANES
    cell_rows = cells // LANES
    planes = 3 * levels
    exact = 2 * levels
    pairs_of = levels // 2
    me = lax.axis_index("mesh")
    lev = lax.axis_index("lev")

    def partner(o):
        offset = o + 1 if o < reach else reach - 1 - o
        return {"mesh": lax.rem(me + offset + n_mesh, n_mesh)}

    up = {"lev": lax.rem(lev + 1, n_lev)}
    down = {"lev": lax.rem(lev + n_lev - 1, n_lev)}

    barrier = pltpu.get_barrier_semaphore()
    for o in range(blocks):
        pl.semaphore_signal(barrier, inc=1, device_id=partner(o), device_id_type=MESH)
    pl.semaphore_signal(barrier, inc=1, device_id=up, device_id_type=MESH)
    pl.semaphore_signal(barrier, inc=1, device_id=down, device_id_type=MESH)

    pairs = [
        (ehl_h, ehl), (ehc_h, ehc), (vel_h, vel), (thk_h, thk), (vor_h, vor),
        (eoc_h, eoc), (eoe_h, eoe), (ew_h, ew), (wts_h, wts), (chl_h, chl), (chc_h, chc),
        (coe_h, coe), (invd_h, invd), (wind_h, wind),
    ]
    loads = []
    for i, (src, dst) in enumerate(pairs):
        copy = pltpu.make_async_copy(src, dst, load_sem.at[i])
        copy.start()
        loads.append(copy)
    esend[...] = jnp.zeros_like(esend)
    csend[...] = jnp.zeros_like(csend)
    cell_pick[...] = jnp.zeros_like(cell_pick)

    sublane = lax.broadcasted_iota(jnp.int32, (SUB, LANES), 0)
    lane = lax.broadcasted_iota(jnp.int32, (SUB, LANES), 1)
    blank = jnp.zeros((SUB, LANES), jnp.float32)

    def live(counts):
        most = jnp.zeros((SUB, LANES), jnp.int32)
        for o in range(blocks):
            most = jnp.where(sublane == o, counts[o], most)
        return lane < most

    def field_rows(k):
        return [
            spread(field[l : l + 1, tile(k)]) for field in (vel, thk, vor) for l in range(levels)
        ]

    def table_rows(k):
        rows = [spread(field[l : l + 1, tile(k)]) for field in (vel, vor) for l in range(levels)]
        return rows + [spread(code[i : i + 1, tile(k)]) for i in range(pairs_of)]

    def speed_rows(k):
        return [spread(vel[l : l + 1, tile(k)]) for l in range(levels)]

    def padded_rows(x):
        return jnp.concatenate([x, jnp.zeros((SUB - x.shape[0], LANES), x.dtype)], axis=0)

    def halo_copy(source, target, sent, arrived, o):
        rows = pl.ds(SUB * o, SUB)
        return pltpu.make_async_remote_copy(
            src_ref=source.at[rows],
            dst_ref=target.at[rows],
            send_sem=sent.at[o],
            recv_sem=arrived.at[o],
            device_id=partner(o),
            device_id_type=MESH,
        )

    edge_copies = [halo_copy(esend, erecv, es_sem, er_sem, o) for o in range(blocks)]
    cell_copies = [halo_copy(csend, crecv, cs_sem, cr_sem, o) for o in range(blocks)]
    rim_copies = [
        pltpu.make_async_remote_copy(
            src_ref=vel,
            dst_ref=dst,
            send_sem=ls_sem.at[i],
            recv_sem=lr_sem.at[i],
            device_id=target,
            device_id_type=MESH,
        )
        for i, (dst, target) in enumerate(((below, up), (above, down)))
    ]
    energy_out = pltpu.make_async_copy(energy, energy_h, out_sem.at[0])

    for copy in loads[:5]:
        copy.wait()
    index = padded_rows(ehl[...])
    (packed,) = scan(
        0, edge_rows, field_rows, [(index >> 7, index & 127)], [(blank,) * planes], edge_rows
    )
    alive = live(ehc)
    for p in range(planes):
        block = jnp.where(alive, packed[p], 0.0)
        for o in range(blocks):
            esend[SUB * o + p : SUB * o + p + 1, :] = block[o : o + 1]

    for i in range(pairs_of):
        code[i : i + 1, :] = coded(thk[2 * i : 2 * i + 1, :], thk[2 * i + 1 : 2 * i + 2, :])

    loads[6].wait()

    def unit_lookups(u):
        lookups = []
        for q in range(group):
            index = eoe[0:SUB, tile(u * group + q)]
            lookups.append((index >> 7, index & 127))
        index = jnp.concatenate(
            [eoe[SUB:neoe, tile(u * group + q)] for q in range(group)], axis=0
        )
        lookups.append((index >> 7, index & 127))
        return lookups

    none = (blank,) * exact + (jnp.zeros((SUB, LANES), jnp.int32),) * pairs_of

    def local_unit(u, carry):
        found = scan(
            0, edge_rows, table_rows, unit_lookups(u), [none] * (group + 1), edge_rows
        )
        for g in range(group + 1):
            for p in range(exact):
                near[u, g * exact + p] = found[g][p]
            for i in range(pairs_of):
                near_code[u, g * pairs_of + i] = found[g][exact + i]
        return carry

    def halo_rows(which, codes):
        def load(k):
            start = pl.multiple_of(SUB * (k - edge_rows), SUB)
            rows = erecv[pl.ds(start, SUB), :]
            taken = [spread(rows[p : p + 1]) for p in which]
            if codes:
                rows = code_halo[pl.ds(start, SUB), :]
                taken += [spread(rows[i : i + 1]) for i in range(pairs_of)]
            return taken

        return load

    def energy_rows(k):
        return [spread(energy[l : l + 1, tile(k)]) for l in range(levels)]

    def edges_leave():
        pl.semaphore_wait(barrier, blocks + 2)
        for copy in edge_copies + rim_copies:
            copy.start()

    def energy_step():
        loads[5].wait()
        cell_lookups = []
        for c in range(cell_rows):
            index = padded_rows(eoc[:, c * LANES : (c + 1) * LANES])
            cell_lookups.append((index >> 7, index & 127))
        found = scan(
            0, edge_rows, speed_rows, cell_lookups, [(blank,) * levels] * cell_rows, edge_rows
        )
        for copy in edge_copies:
            copy.wait()
        loads[7].wait()

        for o in range(blocks):
            for i in range(pairs_of):
                first = SUB * o + levels + 2 * i
                code_halo[SUB * o + i : SUB * o + i + 1, :] = coded(
                    erecv[first : first + 1, :], erecv[first + 1 : first + 2, :]
                )

        found = scan(edge_rows, edge_rows + blocks, halo_rows(range(levels), False), cell_lookups, found, blocks)
        for c in range(cell_rows):
            weight = padded_rows(ew[:, c * LANES : (c + 1) * LANES])
            energy[:, c * LANES : (c + 1) * LANES] = jnp.concatenate(
                [total_rows(weight * found[c][l] * found[c][l]) for l in range(levels)], axis=0
            )

        energy_out.start()

        for copy in loads[9:11]:
            copy.wait()
        cell_pick[0:blocks, 0:halo_c] = chl[...]
        index = cell_pick[...]

        (packed,) = scan(
            0, cell_rows, energy_rows, [(index >> 7, index & 127)], [(blank,) * levels], cell_rows
        )
        alive = live(chc)
        for l in range(levels):
            block = jnp.where(alive, packed[l], 0.0)
            for o in range(blocks):
                csend[SUB * o + l : SUB * o + l + 1, :] = block[o : o + 1]
        for copy in cell_copies:
            copy.start()

    def unit_step(u, carry):
        pl.when(u == units // 3)(edges_leave)
        pl.when(u == 2 * units // 3)(energy_step)
        return local_unit(u, carry)

    lax.fori_loop(0, units, unit_step, 0)

    loads[8].wait()

    table_halo = halo_rows(list(range(levels)) + list(range(2 * levels, planes)), True)

    def halo_unit(u, carry):
        found = [
            tuple(near[u, g * exact + p] for p in range(exact))
            + tuple(near_code[u, g * pairs_of + i] for i in range(pairs_of))
            for g in range(group + 1)
        ]
        found = scan(
            edge_rows, edge_rows + blocks, table_halo, unit_lookups(u), found, blocks
        )
        heights = [sum((decoded(f[exact + i]) for i in range(pairs_of)), ()) for f in found]
        cols = [tile(u * group + q) for q in range(group)]
        few = jnp.concatenate([wts[SUB:neoe, c] for c in cols], axis=0)
        tangents = [[] for _ in cols]
        fluxes = [[] for _ in cols]
        for l in range(levels):
            own = [vor[l : l + 1, c] for c in cols]
            speed, potential = found[group][l], found[group][levels + l]
            own_few = jnp.concatenate(
                [jnp.broadcast_to(v, (extra, LANES)) for v in own], axis=0
            )
            moved_few = few * speed
            flux_few = moved_few * heights[group][l] * (0.5 / STEPS) * (own_few + potential)
            for q, c in enumerate(cols):
                speed, potential = found[q][l], found[q][levels + l]
                moved = wts[0:SUB, c] * speed
                flux = moved * heights[q][l] * (0.5 / STEPS) * (spread(own[q]) + potential)
                part = slice(extra * q, extra * (q + 1))
                tangents[q].append(total_rows(moved) + total_rows(moved_few[part]))
                fluxes[q].append(total_rows(flux) + total_rows(flux_few[part]))
        for q, c in enumerate(cols):
            tang[:, c] = jnp.concatenate(tangents[q], axis=0)
            tend[:, c] = jnp.concatenate(fluxes[q], axis=0)
        return carry

    lax.fori_loop(0, units, halo_unit, 0, unroll=2)
    tang_out = pltpu.make_async_copy(tang, tang_h, out_sem.at[1])
    tang_out.start()

    for copy in rim_copies + loads[11:]:
        copy.wait()
    ends = SUB // 2
    end_units = edge_rows // ends
    places = []
    for u in range(end_units):
        index = jnp.concatenate([coe[:, tile(u * ends + q)] for q in range(ends)], axis=0)
        far = index >= cells
        slot = index - cells
        places.append((
            jnp.where(far, cell_rows + slot // halo_c, index >> 7),
            jnp.where(far, slot % halo_c, index & 127),
        ))
    found = scan(
        0, cell_rows, energy_rows, places, [(blank,) * levels] * end_units, cell_rows
    )
    for c in range(edge_rows):
        col = tile(c)
        for l in range(levels):
            if l + 1 < levels:
                over = vel[l + 1 : l + 2, col]
            else:
                over = jnp.where(lev == n_lev - 1, 0.0, above[0:1, col])
            if l > 0:
                under = vel[l - 1 : l, col]
            else:
                under = jnp.where(lev == 0, 0.0, below[levels - 1 : levels, col])
            wind[l : l + 1, col] = -0.5 * wind[l : l + 1, col] * (over - under)

    def received_rows(k):
        start = pl.multiple_of(SUB * (k - cell_rows), SUB)
        rows = crecv[pl.ds(start, SUB), :]
        return [spread(rows[l : l + 1]) for l in range(levels)]

    for copy in cell_copies:
        copy.wait()
    found = scan(cell_rows, cell_rows + blocks, received_rows, places, found, blocks)
    for c in range(edge_rows):
        u, q = c // ends, c % ends
        gradient = jnp.concatenate(
            [
                found[u][l][2 * q + 1 : 2 * q + 2] - found[u][l][2 * q : 2 * q + 1]
                for l in range(levels)
            ],
            axis=0,
        ) * invd[c : c + 1, :]
        tend[:, tile(c)] = (tend[:, tile(c)] - gradient) + wind[:, tile(c)]

    tend_out = pltpu.make_async_copy(tend, tend_h, out_sem.at[2])
    tend_out.start()
    for copy in (energy_out, tang_out, tend_out):
        copy.wait()


def place(*refs):
    *arrays, in_sem, out_sem = refs
    count = len(arrays) // 3
    sources, targets, held = (arrays[i * count : (i + 1) * count] for i in range(3))
    ins = [pltpu.make_async_copy(sources[i], held[i], in_sem.at[i]) for i in range(count)]
    outs = [pltpu.make_async_copy(held[i], targets[i], out_sem.at[i]) for i in range(count)]
    for copy in ins:
        copy.start()
    for arrived, leaving in zip(ins, outs):
        arrived.wait()
        leaving.start()
    for copy in outs:
        copy.wait()


def body(
    velocity,
    thickness,
    vorticity,
    vertical_wind,
    weights_on_edge,
    edges_on_edge,
    edges_on_cell,
    cells_on_edge,
    energy_weight,
    inverse_distance,
    edge_halo_list,
    edge_halo_count,
    cell_halo_list,
    cell_halo_count,
):
    levels, edges = velocity.shape
    cells = edges_on_cell.shape[1]
    blocks = edge_halo_list.shape[0]
    group = SUB // (edges_on_edge.shape[0] - SUB)
    units = edges // (LANES * group)
    args = [
        velocity, thickness, vorticity, vertical_wind, weights_on_edge, edges_on_edge,
        edges_on_cell, cells_on_edge, energy_weight, inverse_distance.reshape(-1, LANES),
        edge_halo_list, edge_halo_count, cell_halo_list, cell_halo_count,
    ]
    held = [
        pltpu.SMEM(a.shape, a.dtype) if a.ndim == 1 else pltpu.VMEM(a.shape, a.dtype) for a in args
    ]
    exchange = pltpu.VMEM((SUB * blocks, LANES), jnp.float32)
    dma = lambda n: pltpu.SemaphoreType.DMA((n,))
    results = (
        jax.ShapeDtypeStruct((levels, edges), jnp.float32),
        jax.ShapeDtypeStruct((levels, edges), jnp.float32),
        jax.ShapeDtypeStruct((levels, cells), jnp.float32),
    )
    anywhere = pl.BlockSpec(memory_space=pl.ANY)
    found = pl.pallas_call(
        functools.partial(kernel, lax.axis_size("mesh"), lax.axis_size("lev")),
        out_shape=results,
        in_specs=[anywhere] * len(args),
        out_specs=(anywhere,) * 3,
        scratch_shapes=held
        + [
            pltpu.VMEM((levels, edges), jnp.float32),
            pltpu.VMEM((levels, edges), jnp.float32),
            pltpu.VMEM((levels, cells), jnp.float32),
            pltpu.VMEM((levels, edges), jnp.float32),
            pltpu.VMEM((levels, edges), jnp.float32),
            exchange, exchange, exchange, exchange,
            pltpu.VMEM((units, (group + 1) * 2 * levels, SUB, LANES), jnp.float32),
            pltpu.VMEM((units, (group + 1) * (levels // 2), SUB, LANES), jnp.int32),
            pltpu.VMEM((levels // 2, edges), jnp.int32),
            pltpu.VMEM((SUB * blocks, LANES), jnp.int32),
            pltpu.VMEM((SUB, LANES), jnp.int32),
            dma(len(args)), dma(blocks), dma(blocks), dma(blocks), dma(blocks), dma(2), dma(2), dma(3),
        ],
        compiler_params=pltpu.CompilerParams(collective_id=0, has_side_effects=True),
    )(*args)
    return pl.pallas_call(
        place,
        out_shape=results,
        in_specs=[anywhere] * 3,
        out_specs=(anywhere,) * 3,
        scratch_shapes=[pltpu.VMEM(r.shape, r.dtype) for r in results] + [dma(3), dma(3)],
    )(*found)


def solution(mesh):
    in_specs = (
        P("lev", "mesh"),
        P("lev", "mesh"),
        P("lev", "mesh"),
        P("lev", "mesh"),
        P(None, "mesh"),
        P(None, "mesh"),
        P(None, "mesh"),
        P(None, "mesh"),
        P(None, "mesh"),
        P("mesh"),
        P("mesh", None),
        P("mesh"),
        P("mesh", None),
        P("mesh"),
    )
    out_specs = (P("lev", "mesh"), P("lev", "mesh"), P("lev", "mesh"))
    return jax.shard_map(body, mesh=mesh, in_specs=in_specs, out_specs=out_specs, check_vma=False)
```

```python
import functools

import jax
import jax.numpy as jnp
from jax import lax
from jax.experimental import pallas as pl
from jax.experimental.pallas import tpu as pltpu
from jax.sharding import PartitionSpec as P

MESH = pl.DeviceIdType.MESH
LANES = 128
STEPS = 32767.0
HALF = 1 << 16
SUB = 8
ALONG_LANES = lax.GatherDimensionNumbers(
    offset_dims=(),
    collapsed_slice_dims=(1,),
    start_index_map=(1,),
    operand_batching_dims=(0,),
    start_indices_batching_dims=(0,),
)


def pick(row, lanes):
    return lax.gather(
        row,
        lanes[..., None],
        ALONG_LANES,
        slice_sizes=(1, 1),
        mode=lax.GatherScatterMode.PROMISE_IN_BOUNDS,
    )


def tile(c):
    return pl.ds(pl.multiple_of(c * LANES, LANES), LANES)


def spread(row):
    return jnp.broadcast_to(row, (SUB, LANES))


def scan(first, last, load_rows, lookups, found, unroll):
    def one(lookup, held):
        row_of, lane_of = lookup

        def step(k, held):
            hit = row_of == k
            return tuple(jnp.where(hit, pick(r, lane_of), h) for r, h in zip(load_rows(k), held))

        return lax.fori_loop(first, last, step, tuple(held), unroll=unroll)

    return tuple(one(lookup, held) for lookup, held in zip(lookups, found))


def coded(low, high):
    low, high = ((h * STEPS + 0.5).astype(jnp.int32) for h in (low, high))
    return low + high * HALF


def decoded(word):
    return (
        (word & (HALF - 1)).astype(jnp.float32),
        lax.shift_right_logical(word, 16).astype(jnp.float32),
    )


def total_rows(x):
    return jnp.sum(x, axis=0, keepdims=True)


def kernel(
    n_mesh,
    n_lev,
    vel_h, thk_h, vor_h, wind_h, wts_h, eoe_h, eoc_h, coe_h, ew_h, invd_h, ehl_h, ehc_h, chl_h, chc_h,
    tend_h, tang_h, energy_h,
    vel, thk, vor, wind, wts, eoe, eoc, coe, ew, invd, ehl, ehc, chl, chc,
    tend, tang, energy, below, above, esend, erecv, csend, crecv, near, near_code, code, code_halo, cell_pick,
    load_sem, es_sem, er_sem, cs_sem, cr_sem, ls_sem, lr_sem, out_sem,
):
    levels, edges = vel.shape
    cells = energy.shape[1]
    blocks = ehl.shape[0]
    reach = blocks // 2
    halo_c = chl.shape[1]
    neoe, neoc = eoe.shape[0], eoc.shape[0]
    extra = neoe - SUB
    group = SUB // extra
    units = edges // (LANES * group)
    edge_rows = edges // LANES
    cell_rows = cells // LANES
    planes = 3 * levels
    exact = 2 * levels
    pairs_of = levels // 2
    me = lax.axis_index("mesh")
    lev = lax.axis_index("lev")

    def partner(o):
        offset = o + 1 if o < reach else reach - 1 - o
        return {"mesh": lax.rem(me + offset + n_mesh, n_mesh)}

    up = {"lev": lax.rem(lev + 1, n_lev)}
    down = {"lev": lax.rem(lev + n_lev - 1, n_lev)}

    barrier = pltpu.get_barrier_semaphore()
    for o in range(blocks):
        pl.semaphore_signal(barrier, inc=1, device_id=partner(o), device_id_type=MESH)
    pl.semaphore_signal(barrier, inc=1, device_id=up, device_id_type=MESH)
    pl.semaphore_signal(barrier, inc=1, device_id=down, device_id_type=MESH)

    pairs = [
        (ehl_h, ehl), (ehc_h, ehc), (vel_h, vel), (thk_h, thk), (vor_h, vor),
        (eoc_h, eoc), (eoe_h, eoe), (ew_h, ew), (wts_h, wts), (chl_h, chl), (chc_h, chc),
        (coe_h, coe), (invd_h, invd), (wind_h, wind),
    ]
    loads = []
    for i, (src, dst) in enumerate(pairs):
        copy = pltpu.make_async_copy(src, dst, load_sem.at[i])
        copy.start()
        loads.append(copy)
    esend[...] = jnp.zeros_like(esend)
    csend[...] = jnp.zeros_like(csend)
    cell_pick[...] = jnp.zeros_like(cell_pick)

    sublane = lax.broadcasted_iota(jnp.int32, (SUB, LANES), 0)
    lane = lax.broadcasted_iota(jnp.int32, (SUB, LANES), 1)
    blank = jnp.zeros((SUB, LANES), jnp.float32)

    def live(counts):
        most = jnp.zeros((SUB, LANES), jnp.int32)
        for o in range(blocks):
            most = jnp.where(sublane == o, counts[o], most)
        return lane < most

    def field_rows(k):
        return [
            spread(field[l : l + 1, tile(k)]) for field in (vel, thk, vor) for l in range(levels)
        ]

    def table_rows(k):
        rows = [spread(field[l : l + 1, tile(k)]) for field in (vel, vor) for l in range(levels)]
        return rows + [spread(code[i : i + 1, tile(k)]) for i in range(pairs_of)]

    def speed_rows(k):
        return [spread(vel[l : l + 1, tile(k)]) for l in range(levels)]

    def padded_rows(x):
        return jnp.concatenate([x, jnp.zeros((SUB - x.shape[0], LANES), x.dtype)], axis=0)

    def halo_copy(source, target, sent, arrived, o):
        rows = pl.ds(SUB * o, SUB)
        return pltpu.make_async_remote_copy(
            src_ref=source.at[rows],
            dst_ref=target.at[rows],
            send_sem=sent.at[o],
            recv_sem=arrived.at[o],
            device_id=partner(o),
            device_id_type=MESH,
        )

    edge_copies = [halo_copy(esend, erecv, es_sem, er_sem, o) for o in range(blocks)]
    cell_copies = [halo_copy(csend, crecv, cs_sem, cr_sem, o) for o in range(blocks)]
    rim_copies = [
        pltpu.make_async_remote_copy(
            src_ref=vel,
            dst_ref=dst,
            send_sem=ls_sem.at[i],
            recv_sem=lr_sem.at[i],
            device_id=target,
            device_id_type=MESH,
        )
        for i, (dst, target) in enumerate(((below, up), (above, down)))
    ]
    energy_out = pltpu.make_async_copy(energy, energy_h, out_sem.at[0])

    for copy in loads[:5]:
        copy.wait()
    index = padded_rows(ehl[...])
    (packed,) = scan(
        0, edge_rows, field_rows, [(index >> 7, index & 127)], [(blank,) * planes], edge_rows
    )
    alive = live(ehc)
    for p in range(planes):
        block = jnp.where(alive, packed[p], 0.0)
        for o in range(blocks):
            esend[SUB * o + p : SUB * o + p + 1, :] = block[o : o + 1]


    def unit_lookups(u):
        lookups = []
        for q in range(group):
            index = eoe[0:SUB, tile(u * group + q)]
            lookups.append((index >> 7, index & 127))
        index = jnp.concatenate(
            [eoe[SUB:neoe, tile(u * group + q)] for q in range(group)], axis=0
        )
        lookups.append((index >> 7, index & 127))
        return lookups

    none = (blank,) * exact + (jnp.zeros((SUB, LANES), jnp.int32),) * pairs_of

    def local_unit(u, carry):
        found = scan(
            0, edge_rows, table_rows, unit_lookups(u), [none] * (group + 1), edge_rows
        )
        for g in range(group + 1):
            for p in range(exact):
                near[u, g * exact + p] = found[g][p]
            for i in range(pairs_of):
                near_code[u, g * pairs_of + i] = found[g][exact + i]
        return carry

    def halo_rows(which, codes):
        def load(k):
            start = pl.multiple_of(SUB * (k - edge_rows), SUB)
            rows = erecv[pl.ds(start, SUB), :]
            taken = [spread(rows[p : p + 1]) for p in which]
            if codes:
                rows = code_halo[pl.ds(start, SUB), :]
                taken += [spread(rows[i : i + 1]) for i in range(pairs_of)]
            return taken

        return load

    def energy_rows(k):
        return [spread(energy[l : l + 1, tile(k)]) for l in range(levels)]

    def edges_leave():
        pl.semaphore_wait(barrier, blocks + 2)
        for copy in edge_copies + rim_copies:
            copy.start()

    def energy_step():
        loads[5].wait()
        cell_lookups = []
        for c in range(cell_rows):
            index = padded_rows(eoc[:, c * LANES : (c + 1) * LANES])
            cell_lookups.append((index >> 7, index & 127))
        found = scan(
            0, edge_rows, speed_rows, cell_lookups, [(blank,) * levels] * cell_rows, edge_rows
        )
        for copy in edge_copies:
            copy.wait()
        loads[7].wait()

        for o in range(blocks):
            for i in range(pairs_of):
                first = SUB * o + levels + 2 * i
                code_halo[SUB * o + i : SUB * o + i + 1, :] = coded(
                    erecv[first : first + 1, :], erecv[first + 1 : first + 2, :]
                )

        found = scan(edge_rows, edge_rows + blocks, halo_rows(range(levels), False), cell_lookups, found, blocks)
        for c in range(cell_rows):
            weight = padded_rows(ew[:, c * LANES : (c + 1) * LANES])
            energy[:, c * LANES : (c + 1) * LANES] = jnp.concatenate(
                [total_rows(weight * found[c][l] * found[c][l]) for l in range(levels)], axis=0
            )

        energy_out.start()

        for copy in loads[9:11]:
            copy.wait()
        cell_pick[0:blocks, 0:halo_c] = chl[...]
        index = cell_pick[...]

        (packed,) = scan(
            0, cell_rows, energy_rows, [(index >> 7, index & 127)], [(blank,) * levels], cell_rows
        )
        alive = live(chc)
        for l in range(levels):
            block = jnp.where(alive, packed[l], 0.0)
            for o in range(blocks):
                csend[SUB * o + l : SUB * o + l + 1, :] = block[o : o + 1]
        for copy in cell_copies:
            copy.start()

    def unit_step(u, carry):
        pl.when(u == 2 * units // 3)(energy_step)
        return local_unit(u, carry)

    edges_leave()
    for i in range(pairs_of):
        code[i : i + 1, :] = coded(thk[2 * i : 2 * i + 1, :], thk[2 * i + 1 : 2 * i + 2, :])
    loads[6].wait()
    lax.fori_loop(0, units, unit_step, 0)

    loads[8].wait()

    table_halo = halo_rows(list(range(levels)) + list(range(2 * levels, planes)), True)

    def halo_unit(u, carry):
        found = [
            tuple(near[u, g * exact + p] for p in range(exact))
            + tuple(near_code[u, g * pairs_of + i] for i in range(pairs_of))
            for g in range(group + 1)
        ]
        found = scan(
            edge_rows, edge_rows + blocks, table_halo, unit_lookups(u), found, blocks
        )
        heights = [sum((decoded(f[exact + i]) for i in range(pairs_of)), ()) for f in found]
        cols = [tile(u * group + q) for q in range(group)]
        few = jnp.concatenate([wts[SUB:neoe, c] for c in cols], axis=0)
        tangents = [[] for _ in cols]
        fluxes = [[] for _ in cols]
        for l in range(levels):
            own = [vor[l : l + 1, c] for c in cols]
            speed, potential = found[group][l], found[group][levels + l]
            own_few = jnp.concatenate(
                [jnp.broadcast_to(v, (extra, LANES)) for v in own], axis=0
            )
            moved_few = few * speed
            flux_few = moved_few * heights[group][l] * (0.5 / STEPS) * (own_few + potential)
            for q, c in enumerate(cols):
                speed, potential = found[q][l], found[q][levels + l]
                moved = wts[0:SUB, c] * speed
                flux = moved * heights[q][l] * (0.5 / STEPS) * (spread(own[q]) + potential)
                part = slice(extra * q, extra * (q + 1))
                tangents[q].append(total_rows(moved) + total_rows(moved_few[part]))
                fluxes[q].append(total_rows(flux) + total_rows(flux_few[part]))
        for q, c in enumerate(cols):
            tang[:, c] = jnp.concatenate(tangents[q], axis=0)
            tend[:, c] = jnp.concatenate(fluxes[q], axis=0)
        return carry

    lax.fori_loop(0, units, halo_unit, 0, unroll=2)
    tang_out = pltpu.make_async_copy(tang, tang_h, out_sem.at[1])
    tang_out.start()

    for copy in rim_copies + loads[11:]:
        copy.wait()
    ends = SUB // 2
    end_units = edge_rows // ends
    places = []
    for u in range(end_units):
        index = jnp.concatenate([coe[:, tile(u * ends + q)] for q in range(ends)], axis=0)
        far = index >= cells
        slot = index - cells
        places.append((
            jnp.where(far, cell_rows + slot // halo_c, index >> 7),
            jnp.where(far, slot % halo_c, index & 127),
        ))
    found = scan(
        0, cell_rows, energy_rows, places, [(blank,) * levels] * end_units, cell_rows
    )
    for c in range(edge_rows):
        col = tile(c)
        for l in range(levels):
            if l + 1 < levels:
                over = vel[l + 1 : l + 2, col]
            else:
                over = jnp.where(lev == n_lev - 1, 0.0, above[0:1, col])
            if l > 0:
                under = vel[l - 1 : l, col]
            else:
                under = jnp.where(lev == 0, 0.0, below[levels - 1 : levels, col])
            wind[l : l + 1, col] = -0.5 * wind[l : l + 1, col] * (over - under)

    def received_rows(k):
        start = pl.multiple_of(SUB * (k - cell_rows), SUB)
        rows = crecv[pl.ds(start, SUB), :]
        return [spread(rows[l : l + 1]) for l in range(levels)]

    for copy in cell_copies:
        copy.wait()
    found = scan(cell_rows, cell_rows + blocks, received_rows, places, found, blocks)
    for c in range(edge_rows):
        u, q = c // ends, c % ends
        gradient = jnp.concatenate(
            [
                found[u][l][2 * q + 1 : 2 * q + 2] - found[u][l][2 * q : 2 * q + 1]
                for l in range(levels)
            ],
            axis=0,
        ) * invd[c : c + 1, :]
        tend[:, tile(c)] = (tend[:, tile(c)] - gradient) + wind[:, tile(c)]

    tend_out = pltpu.make_async_copy(tend, tend_h, out_sem.at[2])
    tend_out.start()
    for copy in (energy_out, tang_out, tend_out):
        copy.wait()


def place(*refs):
    *arrays, in_sem, out_sem = refs
    count = len(arrays) // 3
    sources, targets, held = (arrays[i * count : (i + 1) * count] for i in range(3))
    ins = [pltpu.make_async_copy(sources[i], held[i], in_sem.at[i]) for i in range(count)]
    outs = [pltpu.make_async_copy(held[i], targets[i], out_sem.at[i]) for i in range(count)]
    for copy in ins:
        copy.start()
    for arrived, leaving in zip(ins, outs):
        arrived.wait()
        leaving.start()
    for copy in outs:
        copy.wait()


def body(
    velocity,
    thickness,
    vorticity,
    vertical_wind,
    weights_on_edge,
    edges_on_edge,
    edges_on_cell,
    cells_on_edge,
    energy_weight,
    inverse_distance,
    edge_halo_list,
    edge_halo_count,
    cell_halo_list,
    cell_halo_count,
):
    levels, edges = velocity.shape
    cells = edges_on_cell.shape[1]
    blocks = edge_halo_list.shape[0]
    group = SUB // (edges_on_edge.shape[0] - SUB)
    units = edges // (LANES * group)
    args = [
        velocity, thickness, vorticity, vertical_wind, weights_on_edge, edges_on_edge,
        edges_on_cell, cells_on_edge, energy_weight, inverse_distance.reshape(-1, LANES),
        edge_halo_list, edge_halo_count, cell_halo_list, cell_halo_count,
    ]
    held = [
        pltpu.SMEM(a.shape, a.dtype) if a.ndim == 1 else pltpu.VMEM(a.shape, a.dtype) for a in args
    ]
    exchange = pltpu.VMEM((SUB * blocks, LANES), jnp.float32)
    dma = lambda n: pltpu.SemaphoreType.DMA((n,))
    results = (
        jax.ShapeDtypeStruct((levels, edges), jnp.float32),
        jax.ShapeDtypeStruct((levels, edges), jnp.float32),
        jax.ShapeDtypeStruct((levels, cells), jnp.float32),
    )
    anywhere = pl.BlockSpec(memory_space=pl.ANY)
    found = pl.pallas_call(
        functools.partial(kernel, lax.axis_size("mesh"), lax.axis_size("lev")),
        out_shape=results,
        in_specs=[anywhere] * len(args),
        out_specs=(anywhere,) * 3,
        scratch_shapes=held
        + [
            pltpu.VMEM((levels, edges), jnp.float32),
            pltpu.VMEM((levels, edges), jnp.float32),
            pltpu.VMEM((levels, cells), jnp.float32),
            pltpu.VMEM((levels, edges), jnp.float32),
            pltpu.VMEM((levels, edges), jnp.float32),
            exchange, exchange, exchange, exchange,
            pltpu.VMEM((units, (group + 1) * 2 * levels, SUB, LANES), jnp.float32),
            pltpu.VMEM((units, (group + 1) * (levels // 2), SUB, LANES), jnp.int32),
            pltpu.VMEM((levels // 2, edges), jnp.int32),
            pltpu.VMEM((SUB * blocks, LANES), jnp.int32),
            pltpu.VMEM((SUB, LANES), jnp.int32),
            dma(len(args)), dma(blocks), dma(blocks), dma(blocks), dma(blocks), dma(2), dma(2), dma(3),
        ],
        compiler_params=pltpu.CompilerParams(collective_id=0, has_side_effects=True),
    )(*args)
    return pl.pallas_call(
        place,
        out_shape=results,
        in_specs=[anywhere] * 3,
        out_specs=(anywhere,) * 3,
        scratch_shapes=[pltpu.VMEM(r.shape, r.dtype) for r in results] + [dma(3), dma(3)],
    )(*found)


def solution(mesh):
    in_specs = (
        P("lev", "mesh"),
        P("lev", "mesh"),
        P("lev", "mesh"),
        P("lev", "mesh"),
        P(None, "mesh"),
        P(None, "mesh"),
        P(None, "mesh"),
        P(None, "mesh"),
        P(None, "mesh"),
        P("mesh"),
        P("mesh", None),
        P("mesh"),
        P("mesh", None),
        P("mesh"),
    )
    out_specs = (P("lev", "mesh"), P("lev", "mesh"), P("lev", "mesh"))
    return jax.shard_map(body, mesh=mesh, in_specs=in_specs, out_specs=out_specs, check_vma=False)
```

```python
import functools

import jax
import jax.numpy as jnp
from jax import lax
from jax.experimental import pallas as pl
from jax.experimental.pallas import tpu as pltpu
from jax.sharding import PartitionSpec as P

MESH = pl.DeviceIdType.MESH
LANES = 128
STEPS = 32767.0
HALF = 1 << 16
SUB = 8
ALONG_LANES = lax.GatherDimensionNumbers(
    offset_dims=(),
    collapsed_slice_dims=(1,),
    start_index_map=(1,),
    operand_batching_dims=(0,),
    start_indices_batching_dims=(0,),
)


def pick(row, lanes):
    return lax.gather(
        row,
        lanes[..., None],
        ALONG_LANES,
        slice_sizes=(1, 1),
        mode=lax.GatherScatterMode.PROMISE_IN_BOUNDS,
    )


def tile(c):
    return pl.ds(pl.multiple_of(c * LANES, LANES), LANES)


def spread(row):
    return jnp.broadcast_to(row, (SUB, LANES))


def scan(first, last, load_rows, lookups, found, unroll):
    def one(lookup, held):
        row_of, lane_of = lookup

        def step(k, held):
            hit = row_of == k
            return tuple(jnp.where(hit, pick(r, lane_of), h) for r, h in zip(load_rows(k), held))

        return lax.fori_loop(first, last, step, tuple(held), unroll=unroll)

    return tuple(one(lookup, held) for lookup, held in zip(lookups, found))


def coded(low, high):
    low, high = ((h * STEPS + 0.5).astype(jnp.int32) for h in (low, high))
    return low + high * HALF


def decoded(word):
    return (
        (word & (HALF - 1)).astype(jnp.float32),
        lax.shift_right_logical(word, 16).astype(jnp.float32),
    )


def total_rows(x):
    return jnp.sum(x, axis=0, keepdims=True)


def kernel(
    n_mesh,
    n_lev,
    vel_h, thk_h, vor_h, wind_h, wts_h, eoe_h, eoc_h, ew_h, ehl_h, ehc_h, chl_h, chc_h,
    tend_h, tang_h, energy_h, crecv,
    vel, thk, vor, wind, wts, eoe, eoc, ew, ehl, ehc, chl, chc,
    tend, tang, energy, below, above, esend, erecv, csend, near, near_code, code, code_halo, cell_pick,
    load_sem, es_sem, er_sem, cs_sem, cr_sem, ls_sem, lr_sem, out_sem,
):
    levels, edges = vel.shape
    cells = energy.shape[1]
    blocks = ehl.shape[0]
    reach = blocks // 2
    halo_c = chl.shape[1]
    neoe, neoc = eoe.shape[0], eoc.shape[0]
    extra = neoe - SUB
    group = SUB // extra
    units = edges // (LANES * group)
    edge_rows = edges // LANES
    cell_rows = cells // LANES
    planes = 3 * levels
    exact = 2 * levels
    pairs_of = levels // 2
    me = lax.axis_index("mesh")
    lev = lax.axis_index("lev")

    order = sorted(range(blocks), key=lambda o: o % reach)

    def partner(o):
        offset = o + 1 if o < reach else reach - 1 - o
        return {"mesh": lax.rem(me + offset + n_mesh, n_mesh)}

    up = {"lev": lax.rem(lev + 1, n_lev)}
    down = {"lev": lax.rem(lev + n_lev - 1, n_lev)}

    barrier = pltpu.get_barrier_semaphore()
    for o in order:
        pl.semaphore_signal(barrier, inc=1, device_id=partner(o), device_id_type=MESH)
    pl.semaphore_signal(barrier, inc=1, device_id=up, device_id_type=MESH)
    pl.semaphore_signal(barrier, inc=1, device_id=down, device_id_type=MESH)

    pairs = [
        (ehl_h, ehl), (ehc_h, ehc), (vel_h, vel), (thk_h, thk), (vor_h, vor),
        (eoc_h, eoc), (eoe_h, eoe), (ew_h, ew), (wts_h, wts), (chl_h, chl), (chc_h, chc),
        (wind_h, wind),
    ]
    loads = []
    for i, (src, dst) in enumerate(pairs):
        copy = pltpu.make_async_copy(src, dst, load_sem.at[i])
        copy.start()
        loads.append(copy)
    esend[...] = jnp.zeros_like(esend)
    csend[...] = jnp.zeros_like(csend)
    cell_pick[...] = jnp.zeros_like(cell_pick)

    sublane = lax.broadcasted_iota(jnp.int32, (SUB, LANES), 0)
    lane = lax.broadcasted_iota(jnp.int32, (SUB, LANES), 1)
    blank = jnp.zeros((SUB, LANES), jnp.float32)

    def live(counts):
        most = jnp.zeros((SUB, LANES), jnp.int32)
        for o in range(blocks):
            most = jnp.where(sublane == o, counts[o], most)
        return lane < most

    def field_rows(k):
        return [
            spread(field[l : l + 1, tile(k)]) for field in (vel, thk, vor) for l in range(levels)
        ]

    def table_rows(k):
        rows = [spread(field[l : l + 1, tile(k)]) for field in (vel, vor) for l in range(levels)]
        return rows + [spread(code[i : i + 1, tile(k)]) for i in range(pairs_of)]

    def speed_rows(k):
        return [spread(vel[l : l + 1, tile(k)]) for l in range(levels)]

    def padded_rows(x):
        return jnp.concatenate([x, jnp.zeros((SUB - x.shape[0], LANES), x.dtype)], axis=0)

    def halo_copy(source, target, sent, arrived, o):
        rows = pl.ds(SUB * o, SUB)
        return pltpu.make_async_remote_copy(
            src_ref=source.at[rows],
            dst_ref=target.at[rows],
            send_sem=sent.at[o],
            recv_sem=arrived.at[o],
            device_id=partner(o),
            device_id_type=MESH,
        )

    edge_copies = [halo_copy(esend, erecv, es_sem, er_sem, o) for o in order]
    cell_copies = [halo_copy(csend, crecv, cs_sem, cr_sem, o) for o in order]
    rim_copies = [
        pltpu.make_async_remote_copy(
            src_ref=vel,
            dst_ref=dst,
            send_sem=ls_sem.at[i],
            recv_sem=lr_sem.at[i],
            device_id=target,
            device_id_type=MESH,
        )
        for i, (dst, target) in enumerate(((below, up), (above, down)))
    ]
    energy_out = pltpu.make_async_copy(energy, energy_h, out_sem.at[0])

    for copy in loads[:5]:
        copy.wait()
    index = padded_rows(ehl[...])
    (packed,) = scan(
        0, edge_rows, field_rows, [(index >> 7, index & 127)], [(blank,) * planes], edge_rows
    )
    alive = live(ehc)
    for p in range(planes):
        block = jnp.where(alive, packed[p], 0.0)
        for o in range(blocks):
            esend[SUB * o + p : SUB * o + p + 1, :] = block[o : o + 1]


    def unit_lookups(u):
        lookups = []
        for q in range(group):
            index = eoe[0:SUB, tile(u * group + q)]
            lookups.append((index >> 7, index & 127))
        index = jnp.concatenate(
            [eoe[SUB:neoe, tile(u * group + q)] for q in range(group)], axis=0
        )
        lookups.append((index >> 7, index & 127))
        return lookups

    none = (blank,) * exact + (jnp.zeros((SUB, LANES), jnp.int32),) * pairs_of

    def local_unit(u, carry):
        found = scan(
            0, edge_rows, table_rows, unit_lookups(u), [none] * (group + 1), edge_rows
        )
        for g in range(group + 1):
            for p in range(exact):
                near[u, g * exact + p] = found[g][p]
            for i in range(pairs_of):
                near_code[u, g * pairs_of + i] = found[g][exact + i]
        return carry

    def halo_rows(which, codes):
        def load(k):
            start = pl.multiple_of(SUB * (k - edge_rows), SUB)
            rows = erecv[pl.ds(start, SUB), :]
            taken = [spread(rows[p : p + 1]) for p in which]
            if codes:
                rows = code_halo[pl.ds(start, SUB), :]
                taken += [spread(rows[i : i + 1]) for i in range(pairs_of)]
            return taken

        return load

    def energy_rows(k):
        return [spread(energy[l : l + 1, tile(k)]) for l in range(levels)]

    def edges_leave():
        pl.semaphore_wait(barrier, blocks + 2)
        for copy in edge_copies + rim_copies:
            copy.start()

    def energy_step():
        loads[5].wait()
        cell_lookups = []
        for c in range(cell_rows):
            index = padded_rows(eoc[:, c * LANES : (c + 1) * LANES])
            cell_lookups.append((index >> 7, index & 127))
        found = scan(
            0, edge_rows, speed_rows, cell_lookups, [(blank,) * levels] * cell_rows, edge_rows
        )
        for copy in edge_copies:
            copy.wait()
        loads[7].wait()

        for o in range(blocks):
            for i in range(pairs_of):
                first = SUB * o + levels + 2 * i
                code_halo[SUB * o + i : SUB * o + i + 1, :] = coded(
                    erecv[first : first + 1, :], erecv[first + 1 : first + 2, :]
                )

        found = scan(edge_rows, edge_rows + blocks, halo_rows(range(levels), False), cell_lookups, found, blocks)
        for c in range(cell_rows):
            weight = padded_rows(ew[:, c * LANES : (c + 1) * LANES])
            energy[:, c * LANES : (c + 1) * LANES] = jnp.concatenate(
                [total_rows(weight * found[c][l] * found[c][l]) for l in range(levels)], axis=0
            )

        energy_out.start()

        for copy in loads[9:11]:
            copy.wait()
        cell_pick[0:blocks, 0:halo_c] = chl[...]
        index = cell_pick[...]

        (packed,) = scan(
            0, cell_rows, energy_rows, [(index >> 7, index & 127)], [(blank,) * levels], cell_rows
        )
        alive = live(chc)
        for l in range(levels):
            block = jnp.where(alive, packed[l], 0.0)
            for o in range(blocks):
                csend[SUB * o + l : SUB * o + l + 1, :] = block[o : o + 1]
        for copy in cell_copies:
            copy.start()

    def unit_step(u, carry):
        pl.when(u == units // 6)(edges_leave)
        pl.when(u == 2 * units // 3)(energy_step)
        return local_unit(u, carry)

    for i in range(pairs_of):
        code[i : i + 1, :] = coded(thk[2 * i : 2 * i + 1, :], thk[2 * i + 1 : 2 * i + 2, :])
    loads[6].wait()
    lax.fori_loop(0, units, unit_step, 0)

    loads[8].wait()

    table_halo = halo_rows(list(range(levels)) + list(range(2 * levels, planes)), True)

    def halo_unit(u, carry):
        found = [
            tuple(near[u, g * exact + p] for p in range(exact))
            + tuple(near_code[u, g * pairs_of + i] for i in range(pairs_of))
            for g in range(group + 1)
        ]
        found = scan(
            edge_rows, edge_rows + blocks, table_halo, unit_lookups(u), found, blocks
        )
        heights = [sum((decoded(f[exact + i]) for i in range(pairs_of)), ()) for f in found]
        cols = [tile(u * group + q) for q in range(group)]
        few = jnp.concatenate([wts[SUB:neoe, c] for c in cols], axis=0)
        tangents = [[] for _ in cols]
        fluxes = [[] for _ in cols]
        for l in range(levels):
            own = [vor[l : l + 1, c] for c in cols]
            speed, potential = found[group][l], found[group][levels + l]
            own_few = jnp.concatenate(
                [jnp.broadcast_to(v, (extra, LANES)) for v in own], axis=0
            )
            moved_few = few * speed
            flux_few = moved_few * heights[group][l] * (0.5 / STEPS) * (own_few + potential)
            for q, c in enumerate(cols):
                speed, potential = found[q][l], found[q][levels + l]
                moved = wts[0:SUB, c] * speed
                flux = moved * heights[q][l] * (0.5 / STEPS) * (spread(own[q]) + potential)
                part = slice(extra * q, extra * (q + 1))
                tangents[q].append(total_rows(moved) + total_rows(moved_few[part]))
                fluxes[q].append(total_rows(flux) + total_rows(flux_few[part]))
        for q, c in enumerate(cols):
            tang[:, c] = jnp.concatenate(tangents[q], axis=0)
            tend[:, c] = jnp.concatenate(fluxes[q], axis=0)
        return carry

    lax.fori_loop(0, units, halo_unit, 0, unroll=2)
    tang_out = pltpu.make_async_copy(tang, tang_h, out_sem.at[1])
    tang_out.start()

    for copy in rim_copies + loads[11:]:
        copy.wait()
    for c in range(edge_rows):
        col = tile(c)
        for l in range(levels):
            if l + 1 < levels:
                over = vel[l + 1 : l + 2, col]
            else:
                over = jnp.where(lev == n_lev - 1, 0.0, above[0:1, col])
            if l > 0:
                under = vel[l - 1 : l, col]
            else:
                under = jnp.where(lev == 0, 0.0, below[levels - 1 : levels, col])
            wind[l : l + 1, col] = -0.5 * wind[l : l + 1, col] * (over - under)
    tend[...] = tend[...] + wind[...]

    tend_out = pltpu.make_async_copy(tend, tend_h, out_sem.at[2])
    tend_out.start()
    for copy in (energy_out, tang_out, tend_out):
        copy.wait()
    for copy in cell_copies:
        copy.wait()


def finish(
    halo_c,
    crecv_h, energy_h, coe_h, invd_h, tend_h, tang_h,
    tend_o, tang_o, energy_o,
    crecv, energy, coe, invd, tend, tang, in_sem, out_sem,
):
    levels, cells = energy.shape
    edge_rows, cell_rows = invd.shape[0], cells // LANES
    blocks = crecv.shape[0] // SUB
    sources = (crecv_h, energy_h, coe_h, invd_h, tend_h, tang_h)
    held = (crecv, energy, coe, invd, tend, tang)
    ins = [
        pltpu.make_async_copy(a, b, in_sem.at[i]) for i, (a, b) in enumerate(zip(sources, held))
    ]
    for copy in ins:
        copy.start()
    outs = [
        pltpu.make_async_copy(a, b, out_sem.at[i])
        for i, (a, b) in enumerate(((energy, energy_o), (tang, tang_o), (tend, tend_o)))
    ]
    for copy in ins:
        copy.wait()
    outs[0].start()
    outs[1].start()

    blank = jnp.zeros((SUB, LANES), jnp.float32)
    ends = SUB // 2
    end_units = edge_rows // ends
    places = []
    for u in range(end_units):
        index = jnp.concatenate([coe[:, tile(u * ends + q)] for q in range(ends)], axis=0)
        far = index >= cells
        slot = index - cells
        places.append((
            jnp.where(far, cell_rows + slot // halo_c, index >> 7),
            jnp.where(far, slot % halo_c, index & 127),
        ))

    def energy_rows(k):
        return [spread(energy[l : l + 1, tile(k)]) for l in range(levels)]

    def received_rows(k):
        start = pl.multiple_of(SUB * (k - cell_rows), SUB)
        rows = crecv[pl.ds(start, SUB), :]
        return [spread(rows[l : l + 1]) for l in range(levels)]

    found = scan(
        0, cell_rows, energy_rows, places, [(blank,) * levels] * end_units, cell_rows
    )
    found = scan(cell_rows, cell_rows + blocks, received_rows, places, found, blocks)
    for c in range(edge_rows):
        u, q = c // ends, c % ends
        gradient = jnp.concatenate(
            [
                found[u][l][2 * q + 1 : 2 * q + 2] - found[u][l][2 * q : 2 * q + 1]
                for l in range(levels)
            ],
            axis=0,
        ) * invd[c : c + 1, :]
        tend[:, tile(c)] = tend[:, tile(c)] - gradient
    outs[2].start()
    for copy in outs:
        copy.wait()


def body(
    velocity,
    thickness,
    vorticity,
    vertical_wind,
    weights_on_edge,
    edges_on_edge,
    edges_on_cell,
    cells_on_edge,
    energy_weight,
    inverse_distance,
    edge_halo_list,
    edge_halo_count,
    cell_halo_list,
    cell_halo_count,
):
    levels, edges = velocity.shape
    cells = edges_on_cell.shape[1]
    blocks = edge_halo_list.shape[0]
    group = SUB // (edges_on_edge.shape[0] - SUB)
    units = edges // (LANES * group)
    args = [
        velocity, thickness, vorticity, vertical_wind, weights_on_edge, edges_on_edge,
        edges_on_cell, energy_weight, edge_halo_list, edge_halo_count, cell_halo_list, cell_halo_count,
    ]
    held = [
        pltpu.SMEM(a.shape, a.dtype) if a.ndim == 1 else pltpu.VMEM(a.shape, a.dtype) for a in args
    ]
    exchange = pltpu.VMEM((SUB * blocks, LANES), jnp.float32)
    landed = jax.ShapeDtypeStruct((SUB * blocks, LANES), jnp.float32)
    dma = lambda n: pltpu.SemaphoreType.DMA((n,))
    results = (
        jax.ShapeDtypeStruct((levels, edges), jnp.float32),
        jax.ShapeDtypeStruct((levels, edges), jnp.float32),
        jax.ShapeDtypeStruct((levels, cells), jnp.float32),
    )
    anywhere = pl.BlockSpec(memory_space=pl.ANY)
    partial, tangent, energy, cell_halo = pl.pallas_call(
        functools.partial(kernel, lax.axis_size("mesh"), lax.axis_size("lev")),
        out_shape=results + (landed,),
        in_specs=[anywhere] * len(args),
        out_specs=(anywhere,) * 4,
        scratch_shapes=held
        + [
            pltpu.VMEM((levels, edges), jnp.float32),
            pltpu.VMEM((levels, edges), jnp.float32),
            pltpu.VMEM((levels, cells), jnp.float32),
            pltpu.VMEM((levels, edges), jnp.float32),
            pltpu.VMEM((levels, edges), jnp.float32),
            exchange, exchange, exchange,
            pltpu.VMEM((units, (group + 1) * 2 * levels, SUB, LANES), jnp.float32),
            pltpu.VMEM((units, (group + 1) * (levels // 2), SUB, LANES), jnp.int32),
            pltpu.VMEM((levels // 2, edges), jnp.int32),
            pltpu.VMEM((SUB * blocks, LANES), jnp.int32),
            pltpu.VMEM((SUB, LANES), jnp.int32),
            dma(len(args)), dma(blocks), dma(blocks), dma(blocks), dma(blocks), dma(2), dma(2), dma(3),
        ],
        compiler_params=pltpu.CompilerParams(collective_id=0, has_side_effects=True),
    )(*args)
    rest = (
        cell_halo, energy, cells_on_edge, inverse_distance.reshape(-1, LANES), partial, tangent
    )
    return pl.pallas_call(
        functools.partial(finish, cell_halo_list.shape[1]),
        out_shape=results,
        in_specs=[anywhere] * len(rest),
        out_specs=(anywhere,) * 3,
        scratch_shapes=[pltpu.VMEM(a.shape, a.dtype) for a in rest] + [dma(len(rest)), dma(3)],
    )(*rest)


def solution(mesh):
    in_specs = (
        P("lev", "mesh"),
        P("lev", "mesh"),
        P("lev", "mesh"),
        P("lev", "mesh"),
        P(None, "mesh"),
        P(None, "mesh"),
        P(None, "mesh"),
        P(None, "mesh"),
        P(None, "mesh"),
        P("mesh"),
        P("mesh", None),
        P("mesh"),
        P("mesh", None),
        P("mesh"),
    )
    out_specs = (P("lev", "mesh"), P("lev", "mesh"), P("lev", "mesh"))
    return jax.shard_map(body, mesh=mesh, in_specs=in_specs, out_specs=out_specs, check_vma=False)
```

```python
import functools

import jax
import jax.numpy as jnp
from jax import lax
from jax.experimental import pallas as pl
from jax.experimental.pallas import tpu as pltpu
from jax.sharding import PartitionSpec as P

MESH = pl.DeviceIdType.MESH
LANES = 128
STEPS = 32767.0
HALF = 1 << 16
SUB = 8
ALONG_LANES = lax.GatherDimensionNumbers(
    offset_dims=(),
    collapsed_slice_dims=(1,),
    start_index_map=(1,),
    operand_batching_dims=(0,),
    start_indices_batching_dims=(0,),
)


def pick(row, lanes):
    return lax.gather(
        row,
        lanes[..., None],
        ALONG_LANES,
        slice_sizes=(1, 1),
        mode=lax.GatherScatterMode.PROMISE_IN_BOUNDS,
    )


def tile(c):
    return pl.ds(pl.multiple_of(c * LANES, LANES), LANES)


def spread(row):
    return jnp.broadcast_to(row, (SUB, LANES))


def scan(first, last, load_rows, lookups, found, unroll):
    def one(lookup, held):
        row_of, lane_of = lookup

        def step(k, held):
            hit = row_of == k
            return tuple(jnp.where(hit, pick(r, lane_of), h) for r, h in zip(load_rows(k), held))

        return lax.fori_loop(first, last, step, tuple(held), unroll=unroll)

    return tuple(one(lookup, held) for lookup, held in zip(lookups, found))


def coded(low, high):
    low, high = ((h * STEPS + 0.5).astype(jnp.int32) for h in (low, high))
    return low + high * HALF


def decoded(word):
    return (
        (word & (HALF - 1)).astype(jnp.float32),
        lax.shift_right_logical(word, 16).astype(jnp.float32),
    )


def total_rows(x):
    return jnp.sum(x, axis=0, keepdims=True)


def kernel(
    n_mesh,
    n_lev,
    vel_h, thk_h, vor_h, wind_h, wts_h, eoe_h, eoc_h, ew_h, ehl_h, ehc_h, chl_h, chc_h,
    tend_h, tang_h, energy_h, crecv,
    vel, thk, vor, wind, wts, eoe, eoc, ew, ehl, ehc, chl, chc,
    tend, tang, energy, below, above, esend, erecv, csend, near, near_code, code, code_halo, cell_pick,
    load_sem, es_sem, er_sem, cs_sem, cr_sem, ls_sem, lr_sem, out_sem,
):
    levels, edges = vel.shape
    cells = energy.shape[1]
    blocks = ehl.shape[0]
    reach = blocks // 2
    halo_c = chl.shape[1]
    neoe, neoc = eoe.shape[0], eoc.shape[0]
    extra = neoe - SUB
    group = SUB // extra
    units = edges // (LANES * group)
    edge_rows = edges // LANES
    cell_rows = cells // LANES
    planes = 3 * levels
    exact = 2 * levels
    pairs_of = levels // 2
    me = lax.axis_index("mesh")
    lev = lax.axis_index("lev")

    order = sorted(range(blocks), key=lambda o: o % reach)

    def partner(o):
        offset = o + 1 if o < reach else reach - 1 - o
        return {"mesh": lax.rem(me + offset + n_mesh, n_mesh)}

    up = {"lev": lax.rem(lev + 1, n_lev)}
    down = {"lev": lax.rem(lev + n_lev - 1, n_lev)}

    barrier = pltpu.get_barrier_semaphore()
    for o in order:
        pl.semaphore_signal(barrier, inc=1, device_id=partner(o), device_id_type=MESH)
    pl.semaphore_signal(barrier, inc=1, device_id=up, device_id_type=MESH)
    pl.semaphore_signal(barrier, inc=1, device_id=down, device_id_type=MESH)

    pairs = [
        (ehl_h, ehl), (ehc_h, ehc), (vel_h, vel), (thk_h, thk), (vor_h, vor),
        (eoc_h, eoc), (eoe_h, eoe), (ew_h, ew), (wts_h, wts), (chl_h, chl), (chc_h, chc),
        (wind_h, wind),
    ]
    loads = []
    for i, (src, dst) in enumerate(pairs):
        copy = pltpu.make_async_copy(src, dst, load_sem.at[i])
        copy.start()
        loads.append(copy)
    esend[...] = jnp.zeros_like(esend)
    csend[...] = jnp.zeros_like(csend)
    cell_pick[...] = jnp.zeros_like(cell_pick)

    sublane = lax.broadcasted_iota(jnp.int32, (SUB, LANES), 0)
    lane = lax.broadcasted_iota(jnp.int32, (SUB, LANES), 1)
    blank = jnp.zeros((SUB, LANES), jnp.float32)

    def live(counts):
        most = jnp.zeros((SUB, LANES), jnp.int32)
        for o in range(blocks):
            most = jnp.where(sublane == o, counts[o], most)
        return lane < most

    def field_rows(k):
        return [
            spread(field[l : l + 1, tile(k)]) for field in (vel, thk, vor) for l in range(levels)
        ]

    def table_rows(k):
        rows = [spread(field[l : l + 1, tile(k)]) for field in (vel, vor) for l in range(levels)]
        return rows + [spread(code[i : i + 1, tile(k)]) for i in range(pairs_of)]

    def speed_rows(k):
        return [spread(vel[l : l + 1, tile(k)]) for l in range(levels)]

    def padded_rows(x):
        return jnp.concatenate([x, jnp.zeros((SUB - x.shape[0], LANES), x.dtype)], axis=0)

    def halo_copy(source, target, sent, arrived, o):
        rows = pl.ds(SUB * o, SUB)
        return pltpu.make_async_remote_copy(
            src_ref=source.at[rows],
            dst_ref=target.at[rows],
            send_sem=sent.at[o],
            recv_sem=arrived.at[o],
            device_id=partner(o),
            device_id_type=MESH,
        )

    edge_copies = [halo_copy(esend, erecv, es_sem, er_sem, o) for o in order]
    cell_copies = [halo_copy(csend, crecv, cs_sem, cr_sem, o) for o in order]
    rim_copies = [
        pltpu.make_async_remote_copy(
            src_ref=vel,
            dst_ref=dst,
            send_sem=ls_sem.at[i],
            recv_sem=lr_sem.at[i],
            device_id=target,
            device_id_type=MESH,
        )
        for i, (dst, target) in enumerate(((below, up), (above, down)))
    ]
    energy_out = pltpu.make_async_copy(energy, energy_h, out_sem.at[0])

    for copy in loads[:5]:
        copy.wait()
    index = padded_rows(ehl[...])
    (packed,) = scan(
        0, edge_rows, field_rows, [(index >> 7, index & 127)], [(blank,) * planes], edge_rows
    )
    alive = live(ehc)
    for p in range(planes):
        block = jnp.where(alive, packed[p], 0.0)
        for o in range(blocks):
            esend[SUB * o + p : SUB * o + p + 1, :] = block[o : o + 1]


    def unit_lookups(u):
        lookups = []
        for q in range(group):
            index = eoe[0:SUB, tile(u * group + q)]
            lookups.append((index >> 7, index & 127))
        index = jnp.concatenate(
            [eoe[SUB:neoe, tile(u * group + q)] for q in range(group)], axis=0
        )
        lookups.append((index >> 7, index & 127))
        return lookups

    none = (blank,) * exact + (jnp.zeros((SUB, LANES), jnp.int32),) * pairs_of

    def local_unit(u, carry):
        found = scan(
            0, edge_rows, table_rows, unit_lookups(u), [none] * (group + 1), edge_rows
        )
        for g in range(group + 1):
            for p in range(exact):
                near[u, g * exact + p] = found[g][p]
            for i in range(pairs_of):
                near_code[u, g * pairs_of + i] = found[g][exact + i]
        return carry

    def halo_rows(which, codes):
        def load(k):
            start = pl.multiple_of(SUB * (k - edge_rows), SUB)
            rows = erecv[pl.ds(start, SUB), :]
            taken = [spread(rows[p : p + 1]) for p in which]
            if codes:
                rows = code_halo[pl.ds(start, SUB), :]
                taken += [spread(rows[i : i + 1]) for i in range(pairs_of)]
            return taken

        return load

    def energy_rows(k):
        return [spread(energy[l : l + 1, tile(k)]) for l in range(levels)]

    def edges_leave():
        pl.semaphore_wait(barrier, blocks + 2)
        for copy in edge_copies + rim_copies:
            copy.start()

    def energy_step():
        loads[5].wait()
        cell_lookups = []
        for c in range(cell_rows):
            index = padded_rows(eoc[:, c * LANES : (c + 1) * LANES])
            cell_lookups.append((index >> 7, index & 127))
        found = scan(
            0, edge_rows, speed_rows, cell_lookups, [(blank,) * levels] * cell_rows, edge_rows
        )
        for copy in edge_copies:
            copy.wait()
        loads[7].wait()

        found = scan(edge_rows, edge_rows + blocks, halo_rows(range(levels), False), cell_lookups, found, blocks)
        for c in range(cell_rows):
            weight = padded_rows(ew[:, c * LANES : (c + 1) * LANES])
            energy[:, c * LANES : (c + 1) * LANES] = jnp.concatenate(
                [total_rows(weight * found[c][l] * found[c][l]) for l in range(levels)], axis=0
            )

        for copy in loads[9:11]:
            copy.wait()
        cell_pick[0:blocks, 0:halo_c] = chl[...]
        index = cell_pick[...]

        (packed,) = scan(
            0, cell_rows, energy_rows, [(index >> 7, index & 127)], [(blank,) * levels], cell_rows
        )
        alive = live(chc)
        for l in range(levels):
            block = jnp.where(alive, packed[l], 0.0)
            for o in range(blocks):
                csend[SUB * o + l : SUB * o + l + 1, :] = block[o : o + 1]
        for copy in cell_copies:
            copy.start()
        energy_out.start()
        for o in range(blocks):
            for i in range(pairs_of):
                first = SUB * o + levels + 2 * i
                code_halo[SUB * o + i : SUB * o + i + 1, :] = coded(
                    erecv[first : first + 1, :], erecv[first + 1 : first + 2, :]
                )

    def unit_step(u, carry):
        pl.when(u == units // 6)(edges_leave)
        pl.when(u == 2 * units // 3)(energy_step)
        return local_unit(u, carry)

    for i in range(pairs_of):
        code[i : i + 1, :] = coded(thk[2 * i : 2 * i + 1, :], thk[2 * i + 1 : 2 * i + 2, :])
    loads[6].wait()
    lax.fori_loop(0, units, unit_step, 0)

    loads[8].wait()

    table_halo = halo_rows(list(range(levels)) + list(range(2 * levels, planes)), True)

    def halo_unit(u, carry):
        found = [
            tuple(near[u, g * exact + p] for p in range(exact))
            + tuple(near_code[u, g * pairs_of + i] for i in range(pairs_of))
            for g in range(group + 1)
        ]
        found = scan(
            edge_rows, edge_rows + blocks, table_halo, unit_lookups(u), found, blocks
        )
        heights = [sum((decoded(f[exact + i]) for i in range(pairs_of)), ()) for f in found]
        cols = [tile(u * group + q) for q in range(group)]
        few = jnp.concatenate([wts[SUB:neoe, c] for c in cols], axis=0)
        tangents = [[] for _ in cols]
        fluxes = [[] for _ in cols]
        for l in range(levels):
            own = [vor[l : l + 1, c] for c in cols]
            speed, potential = found[group][l], found[group][levels + l]
            own_few = jnp.concatenate(
                [jnp.broadcast_to(v, (extra, LANES)) for v in own], axis=0
            )
            moved_few = few * speed
            flux_few = moved_few * heights[group][l] * (0.5 / STEPS) * (own_few + potential)
            for q, c in enumerate(cols):
                speed, potential = found[q][l], found[q][levels + l]
                moved = wts[0:SUB, c] * speed
                flux = moved * heights[q][l] * (0.5 / STEPS) * (spread(own[q]) + potential)
                part = slice(extra * q, extra * (q + 1))
                tangents[q].append(total_rows(moved) + total_rows(moved_few[part]))
                fluxes[q].append(total_rows(flux) + total_rows(flux_few[part]))
        for q, c in enumerate(cols):
            tang[:, c] = jnp.concatenate(tangents[q], axis=0)
            tend[:, c] = jnp.concatenate(fluxes[q], axis=0)
        return carry

    lax.fori_loop(0, units, halo_unit, 0, unroll=2)
    tang_out = pltpu.make_async_copy(tang, tang_h, out_sem.at[1])
    tang_out.start()

    for copy in rim_copies + loads[11:]:
        copy.wait()
    for c in range(edge_rows):
        col = tile(c)
        for l in range(levels):
            if l + 1 < levels:
                over = vel[l + 1 : l + 2, col]
            else:
                over = jnp.where(lev == n_lev - 1, 0.0, above[0:1, col])
            if l > 0:
                under = vel[l - 1 : l, col]
            else:
                under = jnp.where(lev == 0, 0.0, below[levels - 1 : levels, col])
            wind[l : l + 1, col] = -0.5 * wind[l : l + 1, col] * (over - under)
    tend[...] = tend[...] + wind[...]

    tend_out = pltpu.make_async_copy(tend, tend_h, out_sem.at[2])
    tend_out.start()
    for copy in (energy_out, tang_out, tend_out):
        copy.wait()
    for copy in cell_copies:
        copy.wait()


def finish(
    halo_c,
    crecv_h, energy_h, coe_h, invd_h, tend_h, tang_h,
    tend_o, tang_o, energy_o,
    crecv, energy, coe, invd, tend, tang, in_sem, out_sem,
):
    levels, cells = energy.shape
    edge_rows, cell_rows = invd.shape[0], cells // LANES
    blocks = crecv.shape[0] // SUB
    sources = (crecv_h, energy_h, coe_h, invd_h, tend_h, tang_h)
    held = (crecv, energy, coe, invd, tend, tang)
    ins = [
        pltpu.make_async_copy(a, b, in_sem.at[i]) for i, (a, b) in enumerate(zip(sources, held))
    ]
    for copy in ins:
        copy.start()
    outs = [
        pltpu.make_async_copy(a, b, out_sem.at[i])
        for i, (a, b) in enumerate(((energy, energy_o), (tang, tang_o), (tend, tend_o)))
    ]
    for copy in ins:
        copy.wait()
    outs[0].start()
    outs[1].start()

    blank = jnp.zeros((SUB, LANES), jnp.float32)
    ends = SUB // 2
    end_units = edge_rows // ends
    places = []
    for u in range(end_units):
        index = jnp.concatenate([coe[:, tile(u * ends + q)] for q in range(ends)], axis=0)
        far = index >= cells
        slot = index - cells
        places.append((
            jnp.where(far, cell_rows + slot // halo_c, index >> 7),
            jnp.where(far, slot % halo_c, index & 127),
        ))

    def energy_rows(k):
        return [spread(energy[l : l + 1, tile(k)]) for l in range(levels)]

    def received_rows(k):
        start = pl.multiple_of(SUB * (k - cell_rows), SUB)
        rows = crecv[pl.ds(start, SUB), :]
        return [spread(rows[l : l + 1]) for l in range(levels)]

    found = scan(
        0, cell_rows, energy_rows, places, [(blank,) * levels] * end_units, cell_rows
    )
    found = scan(cell_rows, cell_rows + blocks, received_rows, places, found, blocks)
    for c in range(edge_rows):
        u, q = c // ends, c % ends
        gradient = jnp.concatenate(
            [
                found[u][l][2 * q + 1 : 2 * q + 2] - found[u][l][2 * q : 2 * q + 1]
                for l in range(levels)
            ],
            axis=0,
        ) * invd[c : c + 1, :]
        tend[:, tile(c)] = tend[:, tile(c)] - gradient
    outs[2].start()
    for copy in outs:
        copy.wait()


def body(
    velocity,
    thickness,
    vorticity,
    vertical_wind,
    weights_on_edge,
    edges_on_edge,
    edges_on_cell,
    cells_on_edge,
    energy_weight,
    inverse_distance,
    edge_halo_list,
    edge_halo_count,
    cell_halo_list,
    cell_halo_count,
):
    levels, edges = velocity.shape
    cells = edges_on_cell.shape[1]
    blocks = edge_halo_list.shape[0]
    group = SUB // (edges_on_edge.shape[0] - SUB)
    units = edges // (LANES * group)
    args = [
        velocity, thickness, vorticity, vertical_wind, weights_on_edge, edges_on_edge,
        edges_on_cell, energy_weight, edge_halo_list, edge_halo_count, cell_halo_list, cell_halo_count,
    ]
    held = [
        pltpu.SMEM(a.shape, a.dtype) if a.ndim == 1 else pltpu.VMEM(a.shape, a.dtype) for a in args
    ]
    exchange = pltpu.VMEM((SUB * blocks, LANES), jnp.float32)
    landed = jax.ShapeDtypeStruct((SUB * blocks, LANES), jnp.float32)
    dma = lambda n: pltpu.SemaphoreType.DMA((n,))
    results = (
        jax.ShapeDtypeStruct((levels, edges), jnp.float32),
        jax.ShapeDtypeStruct((levels, edges), jnp.float32),
        jax.ShapeDtypeStruct((levels, cells), jnp.float32),
    )
    anywhere = pl.BlockSpec(memory_space=pl.ANY)
    partial, tangent, energy, cell_halo = pl.pallas_call(
        functools.partial(kernel, lax.axis_size("mesh"), lax.axis_size("lev")),
        out_shape=results + (landed,),
        in_specs=[anywhere] * len(args),
        out_specs=(anywhere,) * 4,
        scratch_shapes=held
        + [
            pltpu.VMEM((levels, edges), jnp.float32),
            pltpu.VMEM((levels, edges), jnp.float32),
            pltpu.VMEM((levels, cells), jnp.float32),
            pltpu.VMEM((levels, edges), jnp.float32),
            pltpu.VMEM((levels, edges), jnp.float32),
            exchange, exchange, exchange,
            pltpu.VMEM((units, (group + 1) * 2 * levels, SUB, LANES), jnp.float32),
            pltpu.VMEM((units, (group + 1) * (levels // 2), SUB, LANES), jnp.int32),
            pltpu.VMEM((levels // 2, edges), jnp.int32),
            pltpu.VMEM((SUB * blocks, LANES), jnp.int32),
            pltpu.VMEM((SUB, LANES), jnp.int32),
            dma(len(args)), dma(blocks), dma(blocks), dma(blocks), dma(blocks), dma(2), dma(2), dma(3),
        ],
        compiler_params=pltpu.CompilerParams(collective_id=0, has_side_effects=True),
    )(*args)
    rest = (
        cell_halo, energy, cells_on_edge, inverse_distance.reshape(-1, LANES), partial, tangent
    )
    return pl.pallas_call(
        functools.partial(finish, cell_halo_list.shape[1]),
        out_shape=results,
        in_specs=[anywhere] * len(rest),
        out_specs=(anywhere,) * 3,
        scratch_shapes=[pltpu.VMEM(a.shape, a.dtype) for a in rest] + [dma(len(rest)), dma(3)],
    )(*rest)


def solution(mesh):
    in_specs = (
        P("lev", "mesh"),
        P("lev", "mesh"),
        P("lev", "mesh"),
        P("lev", "mesh"),
        P(None, "mesh"),
        P(None, "mesh"),
        P(None, "mesh"),
        P(None, "mesh"),
        P(None, "mesh"),
        P("mesh"),
        P("mesh", None),
        P("mesh"),
        P("mesh", None),
        P("mesh"),
    )
    out_specs = (P("lev", "mesh"), P("lev", "mesh"), P("lev", "mesh"))
    return jax.shard_map(body, mesh=mesh, in_specs=in_specs, out_specs=out_specs, check_vma=False)
```
